128 devices in a mesh: ctx: 16 (over z, y), chan: 8 (over x, core).
Axes of the slice: x: 4, y: 4, z: 4, core: 2. Of those that a mesh axis runs over, the one named last changes fastest.
Arguments:
- query_proj: bfloat16 [2048, 8192], P('ctx', 'chan'), may hold values from -6 to 6
- key_proj: bfloat16 [2048, 8192], P('ctx', 'chan'), may hold values from -6 to 6
- value_proj: bfloat16 [2048, 8192], P('ctx', 'chan'), may hold values from -6 to 6
- filters: bfloat16 [8192, 128], P('chan'), may hold values from -0.5 to 0.5
- out_weight: bfloat16 [8192, 8192], P('chan'), may hold values from -0.0625 to 0.0625
- cotangent: bfloat16 [2048, 8192], P('ctx', 'chan'), may hold values from -6 to 6
Outputs:
- mixed: bfloat16 [2048, 8192], P('ctx', 'chan')
- grad_query: bfloat16 [2048, 8192], P('ctx', 'chan')
- grad_key: bfloat16 [2048, 8192], P('ctx', 'chan')
- grad_value: bfloat16 [2048, 8192], P('ctx', 'chan')
- grad_filters: float32 [8192, 128], P('chan')
- grad_weight: bfloat16 [8192, 8192], P('chan', 'ctx')
The draws below stay inside these ranges and needn't reach their ends.
All inputs are finite; a program needn't handle non-finite values.
Results may differ from the reference program's by a relative error of at most 0.019.
Values may be sent and summed in bfloat16 or wider, within the bound.
A program may use at most 128 MiB of HBM per device.

```python
import jax
import jax.numpy as jnp
from jax import lax

D = 8192
TAPS = 128
TOK_DEV = 128
TOKENS = 2048
N_CTX = 16


def with_spikes(drawn, own_key, source, target, shards_of, factor):
    def block_of(dim):
        return (jnp.arange(drawn.shape[dim]) // (drawn.shape[dim] // shards_of)).reshape((-1,) + (1,) * (drawn.ndim - 1 - dim))

    one_side = jax.random.permutation(own_key, shards_of)[block_of(target)]
    second = (block_of(target) + shards_of // 2) % shards_of
    return jnp.where((block_of(source) == one_side) | (block_of(source) == second), factor * drawn, drawn)


def steps_of(stream_key, shape, pieces, smallest, largest):
    def one(position, parts):
        heights = jax.random.uniform(jax.random.fold_in(jax.random.fold_in(stream_key, 6), position), (parts,), jnp.float32, smallest / len(pieces), largest / len(pieces))
        return jnp.repeat(jnp.exp(heights), shape[position] // parts).reshape((-1,) + (1,) * (len(shape) - position - 1))

    factor_of = one(*pieces[0])
    for cut in pieces[1:]:
        factor_of = factor_of * one(*cut)
    return factor_of


def scatter_about(rng, dims, width, limit, pieces=(), held_as=jnp.bfloat16):
    values = width * jax.random.normal(rng, dims, jnp.float32)
    if pieces:
        values = values * steps_of(rng, dims, pieces, -0.22, 0.18)
    return jnp.clip(values, -limit, limit).astype(held_as)


def bell_draw_with(rng, extent, scale, limit, pieces, heavy, kind=jnp.bfloat16):
    values = scale * jax.random.normal(rng, extent, jnp.float32)
    if pieces:
        values = values * steps_of(rng, extent, pieces, -0.22, 0.18)
    return jnp.clip(with_spikes(values, jax.random.fold_in(rng, 3), *heavy), -limit, limit).astype(kind)


def setup_inputs(seed: int = 0) -> dict:
    streams_of = jax.random.split(jax.random.key(seed), 7)
    query_proj = scatter_about(streams_of[0], (TOKENS, D), 1.0, 6.0, ((0, 16), (1, 8)))
    key_proj = scatter_about(streams_of[1], (TOKENS, D), 1.0, 6.0, ((0, 16), (1, 8)))
    value_proj = scatter_about(streams_of[2], (TOKENS, D), 1.0, 6.0, ((0, 16), (1, 8)))
    filters = scatter_about(streams_of[3], (D, TAPS), TAPS ** -0.5, 0.5, ((0, 8),))
    out_weight = scatter_about(streams_of[4], (D, D), D ** -0.5, 0.0625, ((0, 8),))
    cotangent = bell_draw_with(streams_of[5], (TOKENS, D), 1.0, 6.0, ((0, 16), (1, 8)), (0, 1, 16, 2.0))
    return dict(query_proj=query_proj, key_proj=key_proj, value_proj=value_proj, filters=filters, out_weight=out_weight, cotangent=cotangent)


def reference(query_proj, key_proj, value_proj, filters, out_weight, cotangent):
    taps_t = filters.astype(jnp.float32).T
    product = (key_proj.astype(jnp.float32) * value_proj.astype(jnp.float32)).astype(jnp.bfloat16)
    padded = jnp.concatenate([jnp.zeros((TAPS - 1, D), jnp.float32), product.astype(jnp.float32)], axis=0)

    def add_tap(offset, running):
        start = (TAPS - 1 - offset).astype(jnp.int32)
        return running + lax.dynamic_slice_in_dim(padded, start, TOKENS, 0) * taps_t[offset]

    filtered = lax.fori_loop(0, TAPS, add_tap, jnp.zeros((TOKENS, D), jnp.float32))
    gated_rows = (query_proj.astype(jnp.float32) * filtered).astype(jnp.bfloat16)
    mixed = jnp.dot(gated_rows, out_weight, preferred_element_type=jnp.float32).astype(jnp.bfloat16)
    grad_gated = jnp.dot(cotangent, out_weight.T, preferred_element_type=jnp.float32)
    grad_query = (grad_gated * filtered).astype(jnp.bfloat16)
    grad_filtered = (grad_gated * query_proj.astype(jnp.float32)).astype(jnp.bfloat16)
    after = jnp.concatenate([grad_filtered.astype(jnp.float32), jnp.zeros((TAPS - 1, D), jnp.float32)], axis=0)

    def add_back(offset, running):
        start = offset.astype(jnp.int32)
        return running + lax.dynamic_slice_in_dim(after, start, TOKENS, 0) * taps_t[offset]

    grad_product = lax.fori_loop(0, TAPS, add_back, jnp.zeros((TOKENS, D), jnp.float32))
    grad_key = (grad_product * value_proj.astype(jnp.float32)).astype(jnp.bfloat16)
    grad_value = (grad_product * key_proj.astype(jnp.float32)).astype(jnp.bfloat16)
    grad_float = grad_filtered.astype(jnp.float32)

    def one_tap(offset):
        start = (TAPS - 1 - offset).astype(jnp.int32)
        return jnp.sum(grad_float * lax.dynamic_slice_in_dim(padded, start, TOKENS, 0), axis=0)

    grad_filters = lax.map(one_tap, jnp.arange(TAPS, dtype=jnp.int32)).T
    gated_blocks = gated_rows.reshape(N_CTX, TOK_DEV, D)
    cot_blocks = cotangent.reshape(N_CTX, TOK_DEV, D)

    def add_block(running, pair):
        block_term = jnp.dot(pair[0].T, pair[1], preferred_element_type=jnp.float32)
        rounded = lax.optimization_barrier(block_term.astype(jnp.bfloat16)).astype(jnp.float32)
        return running + rounded, None

    weight_sum, unused = lax.scan(add_block, jnp.zeros((D, D), jnp.float32), (gated_blocks, cot_blocks))
    grad_weight = weight_sum.astype(jnp.bfloat16)
    return (mixed, grad_query, grad_key, grad_value, grad_filters, grad_weight)
```

```python
import functools

import jax
import jax.numpy as jnp
import numpy as np
from jax import lax
from jax.experimental import pallas as pl
from jax.experimental.pallas import tpu as pltpu
from jax.sharding import PartitionSpec as P

MESH = pl.DeviceIdType.MESH
BF = jnp.bfloat16
F32 = jnp.float32

TOK = 128
CH = 1024
TAPS = 128
N = 256
NCTX = 16
NCHAN = 8
COLS = 512
CC_W = 256
NC = CH // CC_W


def transforms():
    k = np.arange(128, dtype=np.float64)[:, None] + 0.5
    n = np.arange(N, dtype=np.float64)[None, :]
    angle = 2.0 * np.pi * k * n / N
    forward = np.concatenate([np.cos(angle), -np.sin(angle)], axis=0)
    inverse = forward.T / 128.0

    def split(m):
        high = m.astype(jnp.bfloat16)
        low = (m - high.astype(np.float64)).astype(jnp.bfloat16)
        return np.stack([high, low])

    return split(forward), split(inverse)


class Sems:
    def __init__(self):
        self.count = 0

    def take(self, n):
        base = self.count
        self.count += n
        return base


LAYOUT = Sems()
S_HALO = LAYOUT.take(NC)
S_COT = LAYOUT.take(3)
S_COTS = LAYOUT.take(4)
S_A2A = LAYOUT.take(16)
S_X3 = LAYOUT.take(3)
S_X3S = LAYOUT.take(4)
S_AG = LAYOUT.take(NC * 16)
S_MS = LAYOUT.take(4)
S_RS = LAYOUT.take(4)
S_GH = LAYOUT.take(NC)
S_LG = LAYOUT.take(16)
S_FG = LAYOUT.take(16)
N_SEMS = LAYOUT.count


def dot(a, b):
    return jnp.dot(a, b, preferred_element_type=F32)


def dot_nt(a, b):
    return lax.dot_general(a, b, (((1,), (1,)), ((), ())), preferred_element_type=F32)


def kernel(q_in, k_in, v_in, f_in, w_in, cot_in, ef_in, ei_in,
           mixed_o, gq_o, gk_o, gv_o, gf_o, gw_o,
           q, k, v, f, w, cot, ef, ei,
           pext, phat, fhat, ghat, filt, gated, gt, cc,
           part, mself, msib, rsend, rrecv, gg, gfb, gnext, lg, rg, fg, fgo,
           mixed_b, gq_b, gk_b, gv_b, gw_acc, gw_b,
           ld, wl, st, ss, rs):
    s = lax.axis_index("ctx")
    i = lax.axis_index("chan")
    z, y = s // 4, lax.rem(s, 4)
    x, c = i // 2, lax.rem(i, 2)
    sib = x * 2 + (1 - c)

    def ctx_at(dz, dy):
        return lax.rem(z + dz, 4) * 4 + lax.rem(y + dy, 4)

    def chan_at(dx):
        return lax.rem(x + dx, 4) * 2 + c

    barrier = pltpu.get_barrier_semaphore()

    def greet(d, carry):
        pl.semaphore_signal(barrier, inc=1, device_id=(lax.rem(s + d, NCTX), i), device_id_type=MESH)
        return carry

    for dx in (1, 2, 3):
        pl.semaphore_signal(barrier, inc=1, device_id=(s, chan_at(dx)), device_id_type=MESH)
    pl.semaphore_signal(barrier, inc=1, device_id=(s, sib), device_id_type=MESH)
    lax.fori_loop(1, NCTX, greet, 0)

    loads = {}

    def load(name, src, dst, slot):
        loads[name] = pltpu.make_async_copy(src, dst, ld.at[slot])
        loads[name].start()

    load("k", k_in, k, 0)
    load("v", v_in, v, 1)
    load("ef", ef_in, ef, 2)
    load("f", f_in, f, 3)
    load("ei", ei_in, ei, 4)
    load("q", q_in, q, 5)
    load("cot", cot_in, cot.at[i], 6)
    w_loads = []
    for d in range(4):
        columns = pl.ds(d * 2048, 2048)
        copy = pltpu.make_async_copy(w_in.at[:, columns], w.at[:, columns], wl.at[d])
        copy.start()
        w_loads.append(copy)

    def remote(src, dst, slot, ctx, chan):
        return pltpu.make_async_remote_copy(
            src_ref=src, dst_ref=dst, send_sem=ss.at[slot], recv_sem=rs.at[slot],
            device_id=(ctx, chan), device_id_type=MESH)

    sends = []

    def send(src, dst, slot, ctx, chan):
        copy = remote(src, dst, slot, ctx, chan)
        copy.start()
        sends.append(copy)

    def arrived(dst, slot):
        remote(dst, dst, slot, s, sib).wait_recv()

    loads["k"].wait()
    loads["v"].wait()
    pext[pl.ds(TOK, TOK), :] = (k[...].astype(F32) * v[...].astype(F32)).astype(BF)
    loads["ef"].wait()
    loads["f"].wait()
    for n in range(NC):
        taps = f[pl.ds(n * CC_W, CC_W), :]
        fhat[:, pl.ds(n * CC_W, CC_W)] = dot_nt(ef[0, :, 0:TOK], taps) + dot_nt(ef[1, :, 0:TOK], taps)
    loads["ei"].wait()
    loads["q"].wait()
    loads["cot"].wait()

    pl.semaphore_wait(barrier, NCTX - 1 + 4)

    after, before = lax.rem(s + 1, NCTX), lax.rem(s + NCTX - 1, NCTX)
    for n in range(NC):
        columns = pl.ds(n * CC_W, CC_W)
        send(pext.at[pl.ds(TOK, TOK), columns], pext.at[pl.ds(0, TOK), columns], S_HALO + n, after, i)
    for dx in (1, 3, 2):
        send(cot.at[i], cot.at[i], S_COT + dx - 1, s, chan_at(dx))
    send(cot.at[i], cot.at[i], S_COTS, s, sib)

    has_before = jnp.where(s > 0, 1.0, 0.0).astype(BF)
    has_after = jnp.where(s < NCTX - 1, 1.0, 0.0).astype(BF)

    def inverse(rows, spectrum):
        high = spectrum.astype(BF)
        low = (spectrum - high.astype(F32)).astype(BF)
        return dot(ei[0, rows, :], high) + (dot(ei[0, rows, :], low) + dot(ei[1, rows, :], high))

    lower, upper = slice(0, TOK), slice(TOK, N)

    def step_first(n, d):
        return ctx_at(0, d) if n < 2 else ctx_at(d, 0)

    def step_second(n, d):
        return ctx_at(d, 0) if n < 2 else ctx_at(0, d)

    def ag_slot(n, d, e):
        return S_AG + n * 16 + d * 4 + e

    for n in range(NC):
        columns = pl.ds(n * CC_W, CC_W)
        arrived(pext.at[pl.ds(0, TOK), columns], S_HALO + n)
        halo = pext[pl.ds(0, TOK), columns] * has_before
        both = jnp.concatenate([halo, pext[pl.ds(TOK, TOK), columns]], axis=0)
        spectrum = dot(ef[0], both) + dot(ef[1], both)
        phat[:, columns] = spectrum
        taps = fhat[:, columns]
        pr, pi, fr, fi = spectrum[:128], spectrum[128:], taps[:128], taps[128:]
        filtered = inverse(upper, jnp.concatenate([pr * fr - pi * fi, pr * fi + pi * fr], axis=0))
        filt[:, columns] = filtered
        value = q[:, columns].astype(F32) * filtered
        gated[:, columns] = value.astype(BF)
        gt[s, columns, :] = value.T.astype(BF)
        for d in (1, 3, 2):
            send(gt.at[s, columns, :], gt.at[s, columns, :], ag_slot(n, d, 0), step_first(n, d), i)
        for e in (1, 3, 2):
            send(gt.at[s, columns, :], gt.at[s, columns, :], ag_slot(n, 0, e), step_second(n, e), i)

    def forward_gated(n):
        columns = pl.ds(n * CC_W, CC_W)
        for d in (1, 3, 2):
            block = step_first(n, 4 - d)
            arrived(gt.at[block, columns, :], ag_slot(n, d, 0))
            for e in (1, 3, 2):
                send(gt.at[block, columns, :], gt.at[block, columns, :], ag_slot(n, d, e), step_second(n, e), i)

    def forward_cot(dx):
        block = chan_at(4 - dx)
        arrived(cot.at[block], S_COT + dx - 1)
        send(cot.at[block], cot.at[block], S_COTS + dx, s, sib)

    for copy in w_loads:
        copy.wait()

    def wide(d):
        return pl.ds(pl.multiple_of(d * CH, CH), CH)

    def mixed_part(dx):
        own = chan_at(dx)
        other = lax.rem(x + dx, 4) * 2 + (1 - c)
        part[dx] = dot(gated[...], w[:, wide(other)]).astype(BF)
        send(part.at[dx], msib.at[dx], S_MS + dx, s, sib)
        mself[...] = dot(gated[...], w[:, wide(own)])

    def mixed_send(dx):
        arrived(msib.at[dx], S_MS + dx)
        rsend[dx] = (mself[...] + msib[dx].astype(F32)).astype(BF)
        send(rsend.at[dx], rrecv.at[dx], S_RS + dx, s, chan_at(dx))

    mixed_part(2)
    forward_gated(0)
    mixed_send(2)
    mixed_part(1)
    forward_gated(2)
    mixed_send(1)
    forward_cot(1)
    forward_cot(3)
    mixed_part(3)
    forward_gated(1)
    mixed_send(3)
    forward_gated(3)
    mixed_part(0)
    arrived(msib.at[0], S_MS)
    mself[...] = mself[...] + msib[0].astype(F32)
    forward_cot(2)

    gg[...] = dot_nt(cot[i], w[:, wide(i)])
    for dx in (0, 1, 3, 2):
        if dx:
            own = chan_at(4 - dx)
            gg[...] += dot_nt(cot[own], w[:, wide(own)])
        other = lax.rem(x + 4 - dx, 4) * 2 + (1 - c)
        arrived(cot.at[other], S_COTS + dx)
        gg[...] += dot_nt(cot[other], w[:, wide(other)])

    mine = pl.ds(pl.multiple_of(i * 16, 16), 16)

    def columns_of(target):
        return cot.at[target // 2, mine, pl.ds(pl.multiple_of(lax.rem(target, 2) * COLS, COLS), COLS)]

    def spread(d, carry):
        target = lax.rem(s + d, NCTX)
        remote(columns_of(target), cc.at[s, mine, :], S_A2A + d, target, i).start()
        return carry

    lax.fori_loop(1, NCTX, spread, 0)
    keep = pltpu.make_async_copy(columns_of(s), cc.at[s, mine, :], ld.at[7])
    keep.start()

    grad = gg[...]
    gq_b[...] = (grad * filt[...]).astype(BF)
    gfb[...] = (grad * q[...].astype(F32)).astype(BF)
    outs = []

    def store(src, dst, slot):
        copy = pltpu.make_async_copy(src, dst, st.at[slot])
        copy.start()
        outs.append(copy)

    store(gq_b, gq_o, 0)
    for n in range(NC):
        columns = pl.ds(n * CC_W, CC_W)
        send(gfb.at[:, columns], gnext.at[:, columns], S_GH + n, before, i)
    for n in range(NC):
        columns = pl.ds(n * CC_W, CC_W)
        block = gfb[:, columns]
        g = dot(ef[0, :, 0:TOK], block) + dot(ef[1, :, 0:TOK], block)
        ghat[:, columns] = g
        p = phat[:, columns]
        pr, pi, gr, gi = p[:128], p[128:], g[:128], g[128:]
        taps = inverse(upper, jnp.concatenate([gr * pr + gi * pi, gi * pr - gr * pi], axis=0))
        lg[columns, :] = (-taps).T.astype(BF)

    def rows_of(target):
        return pl.ds(pl.multiple_of(target * 64, 64), 64)

    def scatter(d, carry):
        target = lax.rem(s + d, NCTX)
        remote(lg.at[rows_of(target), :], rg.at[s], S_LG + d, target, i).start()
        return carry

    lax.fori_loop(1, NCTX, scatter, 0)
    rg[s] = lg[rows_of(s), :]

    def spread_done(d, carry):
        source = lax.rem(s + NCTX - d, NCTX)
        remote(cc.at[source, mine, :], cc.at[source, mine, :], S_A2A + d, s, sib).wait_recv()
        return carry

    keep.wait()
    lax.fori_loop(1, NCTX, spread_done, 0)

    def share(chan):
        return cc.at[:, pl.ds(pl.multiple_of(chan * 16, 16), 16), :]

    for dx in (1, 3, 2):
        send(share(i), share(i), S_X3 + dx - 1, s, chan_at(dx))
    send(share(i), share(i), S_X3S, s, sib)

    def scatter_done(d, carry):
        source = lax.rem(s + NCTX - d, NCTX)
        remote(rg.at[source], rg.at[source], S_LG + d, s, sib).wait_recv()
        return carry

    lax.fori_loop(1, NCTX, scatter_done, 0)
    total = rg[0].astype(F32)
    for b in range(1, NCTX):
        total = total + rg[b].astype(F32)
    fg[rows_of(s), :] = total.astype(BF)

    def publish(d, carry):
        remote(fg.at[rows_of(s), :], fg.at[rows_of(s), :], S_FG + d, lax.rem(s + d, NCTX), i).start()
        return carry

    lax.fori_loop(1, NCTX, publish, 0)

    for n in range(NC):
        columns = pl.ds(n * CC_W, CC_W)
        arrived(gnext.at[:, columns], S_GH + n)
        block = gnext[:, columns] * has_after
        g = ghat[:, columns] + (dot(ef[0, :, TOK:N], block) + dot(ef[1, :, TOK:N], block))
        taps = fhat[:, columns]
        gr, gi, fr, fi = g[:128], g[128:], taps[:128], taps[128:]
        grad_product = inverse(lower, jnp.concatenate([gr * fr + gi * fi, gi * fr - gr * fi], axis=0))
        gk_b[:, columns] = (grad_product * v[:, columns].astype(F32)).astype(BF)
        gv_b[:, columns] = (grad_product * k[:, columns].astype(F32)).astype(BF)
    store(gk_b, gk_o, 1)
    store(gv_b, gv_o, 2)

    value = mself[...]
    for dx in (1, 3, 2):
        arrived(rrecv.at[dx], S_RS + dx)
        value = value + rrecv[dx].astype(F32)
    mixed_b[...] = value.astype(BF)
    store(mixed_b, mixed_o, 3)

    for dx in (1, 3, 2):
        block = chan_at(4 - dx)
        arrived(share(block), S_X3 + dx - 1)
        send(share(block), share(block), S_X3S + dx, s, sib)

    for n in range(NC):
        columns = pl.ds(n * CC_W, CC_W)
        for e in (1, 3, 2):
            for d in (0, 1, 3, 2):
                first, second = (4 - d) % 4, (4 - e) % 4
                block = ctx_at(second, first) if n < 2 else ctx_at(first, second)
                arrived(gt.at[block, columns, :], ag_slot(n, d, e))
    for dx in range(4):
        other = lax.rem(x + 4 - dx, 4) * 2 + (1 - c)
        arrived(share(other), S_X3S + dx)

    def weight_rows(n, carry):
        rows = pl.ds(pl.multiple_of(n * 256, 256), 256)
        left = jnp.concatenate([gt[b, rows, :] for b in range(NCTX)], axis=1)
        gw_b[rows, :] = dot(left, cc[...].reshape(NCTX * TOK, COLS)).astype(BF)
        return carry

    lax.fori_loop(0, 4, weight_rows, 0)
    store(gw_b, gw_o, 4)

    def publish_done(d, carry):
        rows = rows_of(lax.rem(s + NCTX - d, NCTX))
        remote(fg.at[rows, :], fg.at[rows, :], S_FG + d, s, sib).wait_recv()
        return carry

    lax.fori_loop(1, NCTX, publish_done, 0)
    fgo[...] = fg[...].astype(F32)
    store(fgo, gf_o, 5)

    for copy in sends:
        copy.wait_send()

    def sent(d, carry):
        remote(cc.at[0, mine, :], cc.at[0, mine, :], S_A2A + d, s, sib).wait_send()
        remote(rg.at[0], rg.at[0], S_LG + d, s, sib).wait_send()
        remote(fg.at[rows_of(s), :], fg.at[rows_of(s), :], S_FG + d, s, sib).wait_send()
        return carry

    lax.fori_loop(1, NCTX, sent, 0)
    for copy in outs:
        copy.wait()


def per_device(forward, inverse, query_proj, key_proj, value_proj, filters, out_weight, cotangent):
    sds = jax.ShapeDtypeStruct
    tile = (TOK, CH)
    V = pltpu.VMEM
    anywhere = pl.BlockSpec(memory_space=pl.ANY)
    scratch = [
        V(tile, BF), V(tile, BF), V(tile, BF), V((CH, TAPS), BF), V((CH, NCHAN * CH), BF),
        V((NCHAN,) + tile, BF), V((2, N, N), BF), V((2, N, N), BF),
        V((N, CH), BF), V((N, CH), F32), V((N, CH), F32), V((N, CH), F32), V(tile, F32), V(tile, BF),
        V((NCTX, CH, TOK), BF), V((NCTX, TOK, COLS), BF),
        V((4,) + tile, BF), V(tile, F32), V((4,) + tile, BF), V((4,) + tile, BF), V((4,) + tile, BF),
        V(tile, F32), V(tile, BF), V(tile, BF), V((CH, TAPS), BF), V((NCTX, 64, TAPS), BF),
        V((CH, TAPS), BF), V((CH, TAPS), F32),
        V(tile, BF), V(tile, BF), V(tile, BF), V(tile, BF), V((8, 128), F32), V((CH, COLS), BF),
        pltpu.SemaphoreType.DMA((8,)), pltpu.SemaphoreType.DMA((4,)), pltpu.SemaphoreType.DMA((6,)),
        pltpu.SemaphoreType.DMA((N_SEMS,)), pltpu.SemaphoreType.DMA((N_SEMS,)),
    ]
    return pl.pallas_call(
        kernel,
        out_shape=(
            sds(tile, BF), sds(tile, BF), sds(tile, BF), sds(tile, BF),
            sds((CH, TAPS), F32), sds((CH, COLS), BF),
        ),
        in_specs=[anywhere] * 8,
        out_specs=(anywhere,) * 6,
        scratch_shapes=scratch,
        compiler_params=pltpu.CompilerParams(
            collective_id=0, has_side_effects=True, vmem_limit_bytes=60 * 2**20),
        cost_estimate=pl.CostEstimate(
            flops=7_000_000_000, bytes_accessed=24_000_000, transcendentals=0),
    )(query_proj, key_proj, value_proj, filters, out_weight, cotangent, forward, inverse)


def solution(mesh):
    forward, inverse = transforms()
    placed = (
        P("ctx", "chan"), P("ctx", "chan"), P("ctx", "chan"),
        P("chan", None), P("chan", None), P("ctx", "chan"),
    )

    def body(*args):
        return per_device(jnp.asarray(forward), jnp.asarray(inverse), *args)

    return jax.shard_map(
        body,
        mesh=mesh,
        in_specs=placed,
        out_specs=(
            P("ctx", "chan"), P("ctx", "chan"), P("ctx", "chan"), P("ctx", "chan"),
            P("chan", None), P("chan", "ctx"),
        ),
        check_vma=False,
    )
```

```python
import functools

import jax
import jax.numpy as jnp
import numpy as np
from jax import lax
from jax.experimental import pallas as pl
from jax.experimental.pallas import tpu as pltpu
from jax.sharding import PartitionSpec as P

MESH = pl.DeviceIdType.MESH
BF = jnp.bfloat16
F32 = jnp.float32

TOK = 128
CH = 1024
TAPS = 128
N = 256
NCTX = 16
NCHAN = 8
COLS = 512
CC_W = 256
NC = CH // CC_W


def transforms():
    k = np.arange(128, dtype=np.float64)[:, None] + 0.5
    n = np.arange(N, dtype=np.float64)[None, :]
    angle = 2.0 * np.pi * k * n / N
    forward = np.concatenate([np.cos(angle), -np.sin(angle)], axis=0)
    inverse = forward.T / 128.0

    def split(m):
        high = m.astype(jnp.bfloat16)
        low = (m - high.astype(np.float64)).astype(jnp.bfloat16)
        return np.stack([high, low])

    return split(forward), split(inverse)


class Sems:
    def __init__(self):
        self.count = 0

    def take(self, n):
        base = self.count
        self.count += n
        return base


LAYOUT = Sems()
S_HALO = LAYOUT.take(NC)
S_COT = LAYOUT.take(3)
S_COTS = LAYOUT.take(4)
S_A2A = LAYOUT.take(16)
S_X3 = LAYOUT.take(3)
S_X3S = LAYOUT.take(4)
S_AG = LAYOUT.take(NC * 16)
S_MS = LAYOUT.take(4)
S_RS = LAYOUT.take(4)
S_GH = LAYOUT.take(NC)
S_LG = LAYOUT.take(16)
S_FG = LAYOUT.take(16)
N_SEMS = LAYOUT.count


def dot(a, b):
    return jnp.dot(a, b, preferred_element_type=F32)


def dot_nt(a, b):
    return lax.dot_general(a, b, (((1,), (1,)), ((), ())), preferred_element_type=F32)


def kernel(q_in, k_in, v_in, f_in, w_in, cot_in, ef_in, ei_in,
           mixed_b, gq_b, gk_b, gv_b, fgo, gw_b,
           q, k, v, f, w, cot, ef, ei,
           pext, phat, fhat, ghat, filt, gated, gt, cc,
           part, mself, msib, rsend, rrecv, gg, gfb, gnext, lg, rg, fg,
           ld, wl, ss, rs):
    s = lax.axis_index("ctx")
    i = lax.axis_index("chan")
    z, y = s // 4, lax.rem(s, 4)
    x, c = i // 2, lax.rem(i, 2)
    sib = x * 2 + (1 - c)

    def ctx_at(dz, dy):
        return lax.rem(z + dz, 4) * 4 + lax.rem(y + dy, 4)

    def chan_at(dx):
        return lax.rem(x + dx, 4) * 2 + c

    barrier = pltpu.get_barrier_semaphore()

    def greet(d, carry):
        pl.semaphore_signal(barrier, inc=1, device_id=(lax.rem(s + d, NCTX), i), device_id_type=MESH)
        return carry

    for dx in (1, 2, 3):
        pl.semaphore_signal(barrier, inc=1, device_id=(s, chan_at(dx)), device_id_type=MESH)
    pl.semaphore_signal(barrier, inc=1, device_id=(s, sib), device_id_type=MESH)
    lax.fori_loop(1, NCTX, greet, 0)

    def greet_source(d, carry):
        @pl.when(jnp.logical_or(d != s, s // 2 != i))
        def _():
            pl.semaphore_signal(barrier, inc=1, device_id=(d, s // 2), device_id_type=MESH)

        return carry

    lax.fori_loop(0, NCTX, greet_source, 0)

    loads = {}

    def load(name, src, dst, slot):
        loads[name] = pltpu.make_async_copy(src, dst, ld.at[slot])
        loads[name].start()

    load("k", k_in, k, 0)
    load("v", v_in, v, 1)
    load("ef", ef_in, ef, 2)
    load("f", f_in, f, 3)
    load("ei", ei_in, ei, 4)
    load("q", q_in, q, 5)
    load("cot", cot_in, cot.at[i], 6)
    w_loads = []
    for d in range(4):
        columns = pl.ds(d * 2048, 2048)
        copy = pltpu.make_async_copy(w_in.at[:, columns], w.at[:, columns], wl.at[d])
        copy.start()
        w_loads.append(copy)

    def remote(src, dst, slot, ctx, chan):
        return pltpu.make_async_remote_copy(
            src_ref=src, dst_ref=dst, send_sem=ss.at[slot], recv_sem=rs.at[slot],
            device_id=(ctx, chan), device_id_type=MESH)

    sends = []

    def send(src, dst, slot, ctx, chan):
        copy = remote(src, dst, slot, ctx, chan)
        copy.start()
        sends.append(copy)

    def arrived(dst, slot):
        remote(dst, dst, slot, s, sib).wait_recv()

    loads["k"].wait()
    loads["v"].wait()
    pext[pl.ds(TOK, TOK), :] = (k[...].astype(F32) * v[...].astype(F32)).astype(BF)
    loads["ef"].wait()
    loads["f"].wait()
    for n in range(NC):
        taps = f[pl.ds(n * CC_W, CC_W), :]
        fhat[:, pl.ds(n * CC_W, CC_W)] = dot_nt(ef[0, :, 0:TOK], taps) + dot_nt(ef[1, :, 0:TOK], taps)
    loads["ei"].wait()
    loads["q"].wait()
    loads["cot"].wait()

    pl.semaphore_wait(barrier, NCTX - 1 + 4 + jnp.where(s // 2 == i, 15, 16))

    after, before = lax.rem(s + 1, NCTX), lax.rem(s + NCTX - 1, NCTX)
    for n in range(NC):
        columns = pl.ds(n * CC_W, CC_W)
        send(pext.at[pl.ds(TOK, TOK), columns], pext.at[pl.ds(0, TOK), columns], S_HALO + n, after, i)
    mine = pl.ds(pl.multiple_of(i * 16, 16), 16)

    def spread_copy(d):
        target, chan = 2 * i + d // NCHAN, lax.rem(d, NCHAN)
        rows = pl.ds(pl.multiple_of(chan * 16, 16), 16)
        columns = pl.ds(pl.multiple_of((d // NCHAN) * COLS, COLS), COLS)
        return target, chan, pltpu.make_async_remote_copy(
            src_ref=cot.at[i, rows, columns], dst_ref=cc.at[s, rows, :],
            send_sem=ss.at[S_A2A + d], recv_sem=rs.at[S_A2A + s],
            device_id=(target, chan), device_id_type=MESH)

    def spread(d, carry):
        target, chan, copy = spread_copy(d)

        @pl.when(jnp.logical_or(target != s, chan != i))
        def _():
            copy.start()

        return carry

    def spread_sent(d, carry):
        target, chan, copy = spread_copy(d)

        @pl.when(jnp.logical_or(target != s, chan != i))
        def _():
            copy.wait_send()

        return carry

    def spread_done(b, carry):
        @pl.when(jnp.logical_or(b != s, s // 2 != i))
        def _():
            remote(cc.at[b, mine, :], cc.at[b, mine, :], S_A2A + b, s, sib).wait_recv()

        return carry

    lax.fori_loop(0, 16, spread, 0)

    @pl.when(s // 2 == i)
    def _():
        cc[s, mine, :] = cot[i, mine, pl.ds(pl.multiple_of(lax.rem(s, 2) * COLS, COLS), COLS)]

    for dx in (1, 3, 2):
        send(cot.at[i], cot.at[i], S_COT + dx - 1, s, chan_at(dx))
    send(cot.at[i], cot.at[i], S_COTS, s, sib)

    has_before = jnp.where(s > 0, 1.0, 0.0).astype(BF)
    has_after = jnp.where(s < NCTX - 1, 1.0, 0.0).astype(BF)

    def inverse(rows, spectrum):
        high = spectrum.astype(BF)
        low = (spectrum - high.astype(F32)).astype(BF)
        return dot(ei[0, rows, :], high) + (dot(ei[0, rows, :], low) + dot(ei[1, rows, :], high))

    lower, upper = slice(0, TOK), slice(TOK, N)

    def step_first(n, d):
        return ctx_at(0, d) if n < 2 else ctx_at(d, 0)

    def step_second(n, d):
        return ctx_at(d, 0) if n < 2 else ctx_at(0, d)

    def ag_slot(n, d, e):
        return S_AG + n * 16 + d * 4 + e

    for n in range(NC):
        columns = pl.ds(n * CC_W, CC_W)
        arrived(pext.at[pl.ds(0, TOK), columns], S_HALO + n)
        halo = pext[pl.ds(0, TOK), columns] * has_before
        both = jnp.concatenate([halo, pext[pl.ds(TOK, TOK), columns]], axis=0)
        spectrum = dot(ef[0], both) + dot(ef[1], both)
        phat[:, columns] = spectrum
        taps = fhat[:, columns]
        pr, pi, fr, fi = spectrum[:128], spectrum[128:], taps[:128], taps[128:]
        filtered = inverse(upper, jnp.concatenate([pr * fr - pi * fi, pr * fi + pi * fr], axis=0))
        filt[:, columns] = filtered
        value = q[:, columns].astype(F32) * filtered
        gated[:, columns] = value.astype(BF)
        gt[s, columns, :] = value.T.astype(BF)
        for d in (1, 3, 2):
            send(gt.at[s, columns, :], gt.at[s, columns, :], ag_slot(n, d, 0), step_first(n, d), i)
        for e in (1, 3, 2):
            send(gt.at[s, columns, :], gt.at[s, columns, :], ag_slot(n, 0, e), step_second(n, e), i)

    def forward_gated(n):
        columns = pl.ds(n * CC_W, CC_W)
        for d in (1, 3, 2):
            block = step_first(n, 4 - d)
            arrived(gt.at[block, columns, :], ag_slot(n, d, 0))
            for e in (1, 3, 2):
                send(gt.at[block, columns, :], gt.at[block, columns, :], ag_slot(n, d, e), step_second(n, e), i)

    def forward_cot(dx):
        block = chan_at(4 - dx)
        arrived(cot.at[block], S_COT + dx - 1)
        send(cot.at[block], cot.at[block], S_COTS + dx, s, sib)

    lax.fori_loop(0, NCTX, spread_done, 0)

    def share(chan):
        return cc.at[:, pl.ds(pl.multiple_of(chan * 16, 16), 16), :]

    for dx in (1, 3, 2):
        send(share(i), share(i), S_X3 + dx - 1, s, chan_at(dx))
    send(share(i), share(i), S_X3S, s, sib)

    for copy in w_loads:
        copy.wait()

    def wide(d):
        return pl.ds(pl.multiple_of(d * CH, CH), CH)

    def mixed_part(dx):
        own = chan_at(dx)
        other = lax.rem(x + dx, 4) * 2 + (1 - c)
        part[dx] = dot(gated[...], w[:, wide(other)]).astype(BF)
        send(part.at[dx], msib.at[dx], S_MS + dx, s, sib)
        mself[...] = dot(gated[...], w[:, wide(own)])

    def mixed_send(dx):
        arrived(msib.at[dx], S_MS + dx)
        rsend[dx] = (mself[...] + msib[dx].astype(F32)).astype(BF)
        send(rsend.at[dx], rrecv.at[dx], S_RS + dx, s, chan_at(dx))

    mixed_part(2)
    forward_gated(0)
    mixed_send(2)
    mixed_part(1)
    forward_gated(2)
    mixed_send(1)
    forward_cot(1)
    forward_cot(3)
    mixed_part(3)
    forward_gated(1)
    mixed_send(3)
    forward_gated(3)
    mixed_part(0)
    arrived(msib.at[0], S_MS)
    mself[...] = mself[...] + msib[0].astype(F32)
    forward_cot(2)

    gg[...] = dot_nt(cot[i], w[:, wide(i)])
    for dx in (0, 1, 3, 2):
        if dx:
            own = chan_at(4 - dx)
            gg[...] += dot_nt(cot[own], w[:, wide(own)])
        other = lax.rem(x + 4 - dx, 4) * 2 + (1 - c)
        arrived(cot.at[other], S_COTS + dx)
        gg[...] += dot_nt(cot[other], w[:, wide(other)])

    grad = gg[...]
    gq_b[...] = (grad * filt[...]).astype(BF)
    gfb[...] = (grad * q[...].astype(F32)).astype(BF)
    for n in range(NC):
        columns = pl.ds(n * CC_W, CC_W)
        send(gfb.at[:, columns], gnext.at[:, columns], S_GH + n, before, i)
    for n in range(NC):
        columns = pl.ds(n * CC_W, CC_W)
        block = gfb[:, columns]
        g = dot(ef[0, :, 0:TOK], block) + dot(ef[1, :, 0:TOK], block)
        ghat[:, columns] = g
        p = phat[:, columns]
        pr, pi, gr, gi = p[:128], p[128:], g[:128], g[128:]
        taps = inverse(upper, jnp.concatenate([gr * pr + gi * pi, gi * pr - gr * pi], axis=0))
        lg[columns, :] = (-taps).T.astype(BF)

    def rows_of(target):
        return pl.ds(pl.multiple_of(target * 64, 64), 64)

    def scatter(d, carry):
        target = lax.rem(s + d, NCTX)
        remote(lg.at[rows_of(target), :], rg.at[s], S_LG + d, target, i).start()
        return carry

    lax.fori_loop(1, NCTX, scatter, 0)
    rg[s] = lg[rows_of(s), :]

    def scatter_done(d, carry):
        source = lax.rem(s + NCTX - d, NCTX)
        remote(rg.at[source], rg.at[source], S_LG + d, s, sib).wait_recv()
        return carry

    lax.fori_loop(1, NCTX, scatter_done, 0)
    total = rg[0].astype(F32)
    for b in range(1, NCTX):
        total = total + rg[b].astype(F32)
    fg[rows_of(s), :] = total.astype(BF)

    def publish(d, carry):
        remote(fg.at[rows_of(s), :], fg.at[rows_of(s), :], S_FG + d, lax.rem(s + d, NCTX), i).start()
        return carry

    lax.fori_loop(1, NCTX, publish, 0)

    for n in range(NC):
        columns = pl.ds(n * CC_W, CC_W)
        arrived(gnext.at[:, columns], S_GH + n)
        block = gnext[:, columns] * has_after
        g = ghat[:, columns] + (dot(ef[0, :, TOK:N], block) + dot(ef[1, :, TOK:N], block))
        taps = fhat[:, columns]
        gr, gi, fr, fi = g[:128], g[128:], taps[:128], taps[128:]
        grad_product = inverse(lower, jnp.concatenate([gr * fr + gi * fi, gi * fr - gr * fi], axis=0))
        gk_b[:, columns] = (grad_product * v[:, columns].astype(F32)).astype(BF)
        gv_b[:, columns] = (grad_product * k[:, columns].astype(F32)).astype(BF)

    value = mself[...]
    for dx in (1, 3, 2):
        arrived(rrecv.at[dx], S_RS + dx)
        value = value + rrecv[dx].astype(F32)
    mixed_b[...] = value.astype(BF)

    for dx in (1, 3, 2):
        block = chan_at(4 - dx)
        arrived(share(block), S_X3 + dx - 1)
        send(share(block), share(block), S_X3S + dx, s, sib)

    for n in range(NC):
        columns = pl.ds(n * CC_W, CC_W)
        for e in (1, 3, 2):
            for d in (0, 1, 3, 2):
                first, second = (4 - d) % 4, (4 - e) % 4
                block = ctx_at(second, first) if n < 2 else ctx_at(first, second)
                arrived(gt.at[block, columns, :], ag_slot(n, d, e))
    for dx in range(4):
        other = lax.rem(x + 4 - dx, 4) * 2 + (1 - c)
        arrived(share(other), S_X3S + dx)

    def weight_rows(n, carry):
        rows = pl.ds(pl.multiple_of(n * 256, 256), 256)
        left = jnp.concatenate([gt[b, rows, :] for b in range(NCTX)], axis=1)
        gw_b[rows, :] = dot(left, cc[...].reshape(NCTX * TOK, COLS)).astype(BF)
        return carry

    lax.fori_loop(0, 4, weight_rows, 0)

    def publish_done(d, carry):
        rows = rows_of(lax.rem(s + NCTX - d, NCTX))
        remote(fg.at[rows, :], fg.at[rows, :], S_FG + d, s, sib).wait_recv()
        return carry

    lax.fori_loop(1, NCTX, publish_done, 0)
    fgo[...] = fg[...].astype(F32)

    for copy in sends:
        copy.wait_send()

    def sent(d, carry):
        remote(rg.at[0], rg.at[0], S_LG + d, s, sib).wait_send()
        remote(fg.at[rows_of(s), :], fg.at[rows_of(s), :], S_FG + d, s, sib).wait_send()
        return carry

    lax.fori_loop(1, NCTX, sent, 0)
    lax.fori_loop(0, 16, spread_sent, 0)


def write_out(*refs):
    sources, targets, done = refs[:6], refs[6:12], refs[12]
    copies = [pltpu.make_async_copy(a, b, done.at[n]) for n, (a, b) in enumerate(zip(sources, targets))]
    for copy in copies:
        copy.start()
    for copy in copies:
        copy.wait()


def per_device(forward, inverse, query_proj, key_proj, value_proj, filters, out_weight, cotangent):
    sds = jax.ShapeDtypeStruct
    tile = (TOK, CH)
    V = pltpu.VMEM
    anywhere = pl.BlockSpec(memory_space=pl.ANY)
    scratch = [
        V(tile, BF), V(tile, BF), V(tile, BF), V((CH, TAPS), BF), V((CH, NCHAN * CH), BF),
        V((NCHAN,) + tile, BF), V((2, N, N), BF), V((2, N, N), BF),
        V((N, CH), BF), V((N, CH), F32), V((N, CH), F32), V((N, CH), F32), V(tile, F32), V(tile, BF),
        V((NCTX, CH, TOK), BF), V((NCTX, TOK, COLS), BF),
        V((4,) + tile, BF), V(tile, F32), V((4,) + tile, BF), V((4,) + tile, BF), V((4,) + tile, BF),
        V(tile, F32), V(tile, BF), V(tile, BF), V((CH, TAPS), BF), V((NCTX, 64, TAPS), BF),
        V((CH, TAPS), BF),
        pltpu.SemaphoreType.DMA((8,)), pltpu.SemaphoreType.DMA((4,)),
        pltpu.SemaphoreType.DMA((N_SEMS,)), pltpu.SemaphoreType.DMA((N_SEMS,)),
    ]
    shapes = [(tile, BF)] * 4 + [((CH, TAPS), F32), ((CH, COLS), BF)]
    inside = pl.BlockSpec(memory_space=pltpu.VMEM)
    results = pl.pallas_call(
        kernel,
        out_shape=tuple(V(shape, dtype) for shape, dtype in shapes),
        in_specs=[anywhere] * 8,
        out_specs=(inside,) * 6,
        scratch_shapes=scratch,
        compiler_params=pltpu.CompilerParams(
            collective_id=0, has_side_effects=True, vmem_limit_bytes=50 * 2**20),
        cost_estimate=pl.CostEstimate(
            flops=7_000_000_000, bytes_accessed=24_000_000, transcendentals=0),
    )(query_proj, key_proj, value_proj, filters, out_weight, cotangent, forward, inverse)
    return pl.pallas_call(
        write_out,
        out_shape=tuple(sds(shape, dtype) for shape, dtype in shapes),
        in_specs=[inside] * 6,
        out_specs=(anywhere,) * 6,
        scratch_shapes=[pltpu.SemaphoreType.DMA((6,))],
        compiler_params=pltpu.CompilerParams(vmem_limit_bytes=4 * 2**20),
    )(*results)


def solution(mesh):
    forward, inverse = transforms()
    placed = (
        P("ctx", "chan"), P("ctx", "chan"), P("ctx", "chan"),
        P("chan", None), P("chan", None), P("ctx", "chan"),
    )

    def body(*args):
        return per_device(jnp.asarray(forward), jnp.asarray(inverse), *args)

    return jax.shard_map(
        body,
        mesh=mesh,
        in_specs=placed,
        out_specs=(
            P("ctx", "chan"), P("ctx", "chan"), P("ctx", "chan"), P("ctx", "chan"),
            P("chan", None), P("chan", "ctx"),
        ),
        check_vma=False,
    )
```

```python
import functools

import jax
import jax.numpy as jnp
import numpy as np
from jax import lax
from jax.experimental import pallas as pl
from jax.experimental.pallas import tpu as pltpu
from jax.sharding import PartitionSpec as P

MESH = pl.DeviceIdType.MESH
BF = jnp.bfloat16
F32 = jnp.float32

TOK = 128
CH = 1024
TAPS = 128
N = 256
NCTX = 16
NCHAN = 8
COLS = 512
CC_W = 256
NC = CH // CC_W
ORDER = (0, 2, 1, 3)


def transforms():
    k = np.arange(128, dtype=np.float64)[:, None] + 0.5
    n = np.arange(N, dtype=np.float64)[None, :]
    angle = 2.0 * np.pi * k * n / N
    forward = np.concatenate([np.cos(angle), -np.sin(angle)], axis=0)
    inverse = forward.T / 128.0

    def split(m):
        high = m.astype(jnp.bfloat16)
        low = (m - high.astype(np.float64)).astype(jnp.bfloat16)
        return np.stack([high, low])

    return split(forward), split(inverse)


class Sems:
    def __init__(self):
        self.count = 0

    def take(self, n):
        base = self.count
        self.count += n
        return base


LAYOUT = Sems()
S_HALO = LAYOUT.take(NC)
S_COT = LAYOUT.take(4)
S_COTS = LAYOUT.take(4)
S_A2A = LAYOUT.take(16)
S_X3 = LAYOUT.take(4)
S_X3S = LAYOUT.take(4)
S_AG = LAYOUT.take(NC * 20)
S_MS = LAYOUT.take(4)
S_RS = LAYOUT.take(6)
S_GH = LAYOUT.take(NC)
S_LG = LAYOUT.take(16)
S_FG = LAYOUT.take(16)
N_SEMS = LAYOUT.count


def dot(a, b):
    return jnp.dot(a, b, preferred_element_type=F32)


def dot_nt(a, b):
    return lax.dot_general(a, b, (((1,), (1,)), ((), ())), preferred_element_type=F32)


def kernel(q_in, k_in, v_in, f_in, w_in, cot_in, ef_in, ei_in,
           mixed_b, gq_b, gk_b, gv_b, fgo, gw_b,
           q, k, v, f, w, cot, ef, ei,
           pext, phat, fhat, ghat, filt, gated, gt, cc,
           part, mself, msib, rsend, rrecv, gg, gfb, gnext, lg, rg, fg,
           ld, wl, ss, rs):
    s = lax.axis_index("ctx")
    i = lax.axis_index("chan")
    z, y = s // 4, lax.rem(s, 4)
    x, c = i // 2, lax.rem(i, 2)
    sib = x * 2 + (1 - c)

    def ctx_at(dz, dy):
        return lax.rem(z + dz, 4) * 4 + lax.rem(y + dy, 4)

    def chan_at(dx):
        return lax.rem(x + dx, 4) * 2 + c

    barrier = pltpu.get_barrier_semaphore()

    def greet(d, carry):
        pl.semaphore_signal(barrier, inc=1, device_id=(lax.rem(s + d, NCTX), i), device_id_type=MESH)
        return carry

    for dx in (1, 3):
        pl.semaphore_signal(barrier, inc=1, device_id=(s, chan_at(dx)), device_id_type=MESH)
    pl.semaphore_signal(barrier, inc=1, device_id=(s, sib), device_id_type=MESH)
    lax.fori_loop(1, NCTX, greet, 0)

    def greet_source(d, carry):
        @pl.when(jnp.logical_or(d != s, s // 2 != i))
        def _():
            pl.semaphore_signal(barrier, inc=1, device_id=(d, s // 2), device_id_type=MESH)

        return carry

    lax.fori_loop(0, NCTX, greet_source, 0)

    loads = {}

    def load(name, src, dst, slot):
        loads[name] = pltpu.make_async_copy(src, dst, ld.at[slot])
        loads[name].start()

    load("k", k_in, k, 0)
    load("v", v_in, v, 1)
    load("ef", ef_in, ef, 2)
    load("f", f_in, f, 3)
    load("ei", ei_in, ei, 4)
    load("q", q_in, q, 5)
    load("cot", cot_in, cot.at[i], 6)
    w_loads = []
    for d in range(4):
        columns = pl.ds(d * 2048, 2048)
        copy = pltpu.make_async_copy(w_in.at[:, columns], w.at[:, columns], wl.at[d])
        copy.start()
        w_loads.append(copy)

    def remote(src, dst, slot, ctx, chan):
        return pltpu.make_async_remote_copy(
            src_ref=src, dst_ref=dst, send_sem=ss.at[slot], recv_sem=rs.at[slot],
            device_id=(ctx, chan), device_id_type=MESH)

    sends = []

    def send(src, dst, slot, ctx, chan):
        copy = remote(src, dst, slot, ctx, chan)
        copy.start()
        sends.append(copy)

    def arrived(dst, slot):
        remote(dst, dst, slot, s, sib).wait_recv()

    loads["k"].wait()
    loads["v"].wait()
    pext[pl.ds(TOK, TOK), :] = (k[...].astype(F32) * v[...].astype(F32)).astype(BF)
    loads["ef"].wait()
    loads["f"].wait()
    for n in range(NC):
        taps = f[pl.ds(n * CC_W, CC_W), :]
        fhat[:, pl.ds(n * CC_W, CC_W)] = dot_nt(ef[0, :, 0:TOK], taps) + dot_nt(ef[1, :, 0:TOK], taps)
    loads["ei"].wait()
    loads["q"].wait()
    loads["cot"].wait()

    pl.semaphore_wait(barrier, NCTX - 1 + 3 + jnp.where(s // 2 == i, 15, 16))

    after, before = lax.rem(s + 1, NCTX), lax.rem(s + NCTX - 1, NCTX)
    for n in ORDER:
        columns = pl.ds(n * CC_W, CC_W)
        send(pext.at[pl.ds(TOK, TOK), columns], pext.at[pl.ds(0, TOK), columns], S_HALO + n, after, i)
    mine = pl.ds(pl.multiple_of(i * 16, 16), 16)

    def spread_copy(d):
        target, chan = 2 * i + d // NCHAN, lax.rem(d, NCHAN)
        rows = pl.ds(pl.multiple_of(chan * 16, 16), 16)
        columns = pl.ds(pl.multiple_of((d // NCHAN) * COLS, COLS), COLS)
        return target, chan, pltpu.make_async_remote_copy(
            src_ref=cot.at[i, rows, columns], dst_ref=cc.at[s, rows, :],
            send_sem=ss.at[S_A2A + d], recv_sem=rs.at[S_A2A + s],
            device_id=(target, chan), device_id_type=MESH)

    def spread(d, carry):
        target, chan, copy = spread_copy(d)

        @pl.when(jnp.logical_or(target != s, chan != i))
        def _():
            copy.start()

        return carry

    def spread_sent(d, carry):
        target, chan, copy = spread_copy(d)

        @pl.when(jnp.logical_or(target != s, chan != i))
        def _():
            copy.wait_send()

        return carry

    def spread_done(b, carry):
        @pl.when(jnp.logical_or(b != s, s // 2 != i))
        def _():
            remote(cc.at[b, mine, :], cc.at[b, mine, :], S_A2A + b, s, sib).wait_recv()

        return carry

    lax.fori_loop(0, 16, spread, 0)

    @pl.when(s // 2 == i)
    def _():
        cc[s, mine, :] = cot[i, mine, pl.ds(pl.multiple_of(lax.rem(s, 2) * COLS, COLS), COLS)]

    for m, dx in enumerate((1, 3)):
        send(cot.at[i], cot.at[i], S_COT + m, s, chan_at(dx))
    send(cot.at[i], cot.at[i], S_COTS, s, sib)

    has_before = jnp.where(s > 0, 1.0, 0.0).astype(BF)
    has_after = jnp.where(s < NCTX - 1, 1.0, 0.0).astype(BF)

    def inverse(rows, spectrum):
        high = spectrum.astype(BF)
        low = (spectrum - high.astype(F32)).astype(BF)
        return dot(ei[0, rows, :], high) + (dot(ei[0, rows, :], low) + dot(ei[1, rows, :], high))

    lower, upper = slice(0, TOK), slice(TOK, N)

    def at(n, da, db):
        return ctx_at(db, da) if n < 2 else ctx_at(da, db)

    def gated_send(n, da, db, half, slot, to_a, to_b):
        rows = pl.ds(n * CC_W, CC_W) if half is None else pl.ds(n * CC_W + half * 128, 128)
        block = gt.at[at(n, da, db), rows, :]
        send(block, block, S_AG + n * 20 + slot, at(n, to_a, to_b), i)

    def gated_wait(n, da, db, half, slot):
        rows = pl.ds(n * CC_W, CC_W) if half is None else pl.ds(n * CC_W + half * 128, 128)
        arrived(gt.at[at(n, da, db), rows, :], S_AG + n * 20 + slot)

    def along_second(n, t, da):
        gated_send(n, da, 0, None, 4 + 4 * t, 0, 1)
        gated_send(n, da, 0, None, 5 + 4 * t, 0, 3)

    def gather_own(n):
        gated_send(n, 0, 0, None, 0, 1, 0)
        gated_send(n, 0, 0, None, 1, 3, 0)
        along_second(n, 0, 0)

    def gather_near(n):
        gated_wait(n, 3, 0, None, 0)
        gated_send(n, 3, 0, 0, 2, 1, 0)
        along_second(n, 1, 3)
        gated_wait(n, 1, 0, None, 1)
        gated_send(n, 1, 0, 1, 3, 3, 0)
        along_second(n, 2, 1)

    def gather_far(n):
        gated_wait(n, 2, 0, 0, 2)
        gated_wait(n, 2, 0, 1, 3)
        along_second(n, 3, 2)

    offset_of = (0, 3, 1, 2)

    def gather_pass(n, t):
        da = offset_of[t]
        gated_wait(n, da, 3, None, 4 + 4 * t)
        gated_send(n, da, 3, 0, 6 + 4 * t, 0, 1)
        gated_wait(n, da, 1, None, 5 + 4 * t)
        gated_send(n, da, 1, 1, 7 + 4 * t, 0, 3)

    def gather_end(n, t):
        da = offset_of[t]
        gated_wait(n, da, 2, 0, 6 + 4 * t)
        gated_wait(n, da, 2, 1, 7 + 4 * t)

    def x_near(view, slot, sib_slot):
        for m, (source, target) in enumerate(((3, 1), (1, 3))):
            block = chan_at(source)
            arrived(view(block), slot + m)
            send(view(block, m), view(block, m), slot + 2 + m, s, chan_at(target))
            send(view(block), view(block), sib_slot + 1 + m, s, sib)

    def x_far(view, slot, sib_slot):
        block = chan_at(2)
        for m in range(2):
            arrived(view(block, m), slot + 2 + m)
        send(view(block), view(block), sib_slot + 3, s, sib)

    def cot_view(block, half=None):
        return cot.at[block] if half is None else cot.at[block, pl.ds(half * 64, 64), :]

    def share(block, half=None):
        rows = pl.ds(pl.multiple_of(block * 16, 16), 16)
        return cc.at[:, rows, :] if half is None else cc.at[pl.ds(half * 8, 8), rows, :]

    def mixed_part(dx):
        chip = lax.rem(x + dx, 4)
        both = dot(gated[...], w[:, pl.ds(pl.multiple_of(chip * 2 * CH, 2 * CH), 2 * CH)])
        first, second = both[:, :CH], both[:, CH:]
        part[dx] = jnp.where(c == 0, second, first).astype(BF)
        send(part.at[dx], msib.at[dx], S_MS + dx, s, sib)
        mself[dx] = jnp.where(c == 0, first, second)

    top, bottom = pl.ds(0, 64), pl.ds(64, 64)

    def chip_sum(dx, rows):
        return mself[dx, rows, :] + msib[dx, rows, :].astype(F32)

    def mixed_send(m, dx, value):
        rsend[m] = value.astype(BF)
        send(rsend.at[m], rrecv.at[m], S_RS + m, s, chan_at(dx))

    def mixed_far():
        arrived(msib.at[2], S_MS + 2)
        mixed_send(0, 1, chip_sum(2, top))
        mixed_send(1, 3, chip_sum(2, bottom))

    def mixed_near():
        arrived(msib.at[1], S_MS + 1)
        mixed_send(2, 1, chip_sum(1, bottom))
        arrived(msib.at[3], S_MS + 3)
        mixed_send(3, 3, chip_sum(3, top))

    def mixed_last():
        arrived(rrecv.at[0], S_RS)
        mixed_send(4, 1, chip_sum(1, top) + rrecv[0].astype(F32))
        arrived(rrecv.at[1], S_RS + 1)
        mixed_send(5, 3, chip_sum(3, bottom) + rrecv[1].astype(F32))

    def mixed_end():
        arrived(msib.at[0], S_MS)
        for m in (2, 3, 4, 5):
            arrived(rrecv.at[m], S_RS + m)
        mixed_b[top, :] = (chip_sum(0, top) + rrecv[4].astype(F32) + rrecv[3].astype(F32)).astype(BF)
        mixed_b[bottom, :] = (chip_sum(0, bottom) + rrecv[2].astype(F32) + rrecv[5].astype(F32)).astype(BF)

    def gated_chunk(n):
        columns = pl.ds(n * CC_W, CC_W)
        arrived(pext.at[pl.ds(0, TOK), columns], S_HALO + n)
        halo = pext[pl.ds(0, TOK), columns] * has_before
        both = jnp.concatenate([halo, pext[pl.ds(TOK, TOK), columns]], axis=0)
        spectrum = dot(ef[0], both) + dot(ef[1], both)
        phat[:, columns] = spectrum
        taps = fhat[:, columns]
        pr, pi, fr, fi = spectrum[:128], spectrum[128:], taps[:128], taps[128:]
        filtered = inverse(upper, jnp.concatenate([pr * fr - pi * fi, pr * fi + pi * fr], axis=0))
        filt[:, columns] = filtered
        value = q[:, columns].astype(F32) * filtered
        gated[:, columns] = value.astype(BF)
        gt[s, columns, :] = value.T.astype(BF)

    def share_out():
        lax.fori_loop(0, NCTX, spread_done, 0)
        for m, dx in enumerate((1, 3)):
            send(share(i), share(i), S_X3 + m, s, chan_at(dx))
        send(share(i), share(i), S_X3S, s, sib)

    def grad_gated_part(dx, slot):
        chip = lax.rem(x + dx, 4)
        arrived(cot.at[chip * 2 + (1 - c)], S_COTS + slot)
        row = jnp.concatenate([cot[chip * 2], cot[chip * 2 + 1]], axis=1)
        term = dot_nt(row, w[:, pl.ds(pl.multiple_of(chip * 2 * CH, 2 * CH), 2 * CH)])
        if slot == 0:
            gg[...] = term
        else:
            gg[...] += term

    def gradients():
        grad = gg[...]
        gfb[...] = (grad * q[...].astype(F32)).astype(BF)
        for n in range(NC):
            columns = pl.ds(n * CC_W, CC_W)
            send(gfb.at[:, columns], gnext.at[:, columns], S_GH + n, before, i)
        gq_b[...] = (grad * filt[...]).astype(BF)

    def filter_terms(n):
        columns = pl.ds(n * CC_W, CC_W)
        block = gfb[:, columns]
        g = dot(ef[0, :, 0:TOK], block) + dot(ef[1, :, 0:TOK], block)
        ghat[:, columns] = g
        p = phat[:, columns]
        pr, pi, gr, gi = p[:128], p[128:], g[:128], g[128:]
        taps = inverse(upper, jnp.concatenate([gr * pr + gi * pi, gi * pr - gr * pi], axis=0))
        lg[columns, :] = (-taps).T.astype(BF)

    def rows_of(target):
        return pl.ds(pl.multiple_of(target * 64, 64), 64)

    def scatter(d, carry):
        target = lax.rem(s + d, NCTX)
        remote(lg.at[rows_of(target), :], rg.at[s], S_LG + d, target, i).start()
        return carry

    def scatter_done(d, carry):
        source = lax.rem(s + NCTX - d, NCTX)
        remote(rg.at[source], rg.at[source], S_LG + d, s, sib).wait_recv()
        return carry

    def publish(d, carry):
        remote(fg.at[rows_of(s), :], fg.at[rows_of(s), :], S_FG + d, lax.rem(s + d, NCTX), i).start()
        return carry

    def publish_done(d, carry):
        rows = rows_of(lax.rem(s + NCTX - d, NCTX))
        remote(fg.at[rows, :], fg.at[rows, :], S_FG + d, s, sib).wait_recv()
        return carry

    def filters_out():
        lax.fori_loop(1, NCTX, scatter, 0)
        rg[s] = lg[rows_of(s), :]

    def filters_sum():
        lax.fori_loop(1, NCTX, scatter_done, 0)
        total = rg[0].astype(F32)
        for b in range(1, NCTX):
            total = total + rg[b].astype(F32)
        fg[rows_of(s), :] = total.astype(BF)
        lax.fori_loop(1, NCTX, publish, 0)

    def filters_end():
        lax.fori_loop(1, NCTX, publish_done, 0)
        fgo[...] = fg[...].astype(F32)

    def product_gradient(n):
        columns = pl.ds(n * CC_W, CC_W)
        arrived(gnext.at[:, columns], S_GH + n)
        block = gnext[:, columns] * has_after
        g = ghat[:, columns] + (dot(ef[0, :, TOK:N], block) + dot(ef[1, :, TOK:N], block))
        taps = fhat[:, columns]
        gr, gi, fr, fi = g[:128], g[128:], taps[:128], taps[128:]
        grad_product = inverse(lower, jnp.concatenate([gr * fr + gi * fi, gi * fr - gr * fi], axis=0))
        gk_b[:, columns] = (grad_product * v[:, columns].astype(F32)).astype(BF)
        gv_b[:, columns] = (grad_product * k[:, columns].astype(F32)).astype(BF)

    def share_end():
        for slot, dx in enumerate((0, 3, 1, 2)):
            arrived(share(lax.rem(x + dx, 4) * 2 + (1 - c)), S_X3S + slot)

    def weight_rows(n):
        for t in range(4):
            gather_end(n, t)
        rows = pl.ds(n * CC_W, CC_W)
        left = jnp.concatenate([gt[b, rows, :] for b in range(NCTX)], axis=1)
        gw_b[rows, :] = dot(left, cc[...].reshape(NCTX * TOK, COLS)).astype(BF)

    for copy in w_loads:
        copy.wait()
    grad_gated_part(0, 0)
    for n in ORDER:
        gated_chunk(n)
        gather_own(n)
    x_near(cot_view, S_COT, S_COTS)
    gather_near(0)
    grad_gated_part(3, 1)
    gather_near(2)
    gather_pass(0, 0)
    grad_gated_part(1, 2)
    x_far(cot_view, S_COT, S_COTS)
    share_out()
    gather_near(1)
    gather_far(0)
    gather_pass(2, 0)
    grad_gated_part(2, 3)
    gather_near(3)
    gather_far(2)
    gradients()
    gather_pass(0, 1)
    gather_pass(2, 1)
    for n in range(NC):
        filter_terms(n)
    filters_out()
    gather_pass(1, 0)
    gather_far(1)
    gather_pass(3, 0)
    gather_far(3)
    mixed_part(2)
    gather_pass(0, 2)
    gather_pass(2, 2)
    mixed_far()
    mixed_part(1)
    x_near(share, S_X3, S_X3S)
    gather_pass(0, 3)
    gather_pass(2, 3)
    mixed_part(3)
    mixed_near()
    filters_sum()
    gather_pass(1, 1)
    gather_pass(3, 1)
    mixed_part(0)
    mixed_last()
    x_far(share, S_X3, S_X3S)
    gather_pass(1, 2)
    gather_pass(3, 2)
    for n in range(NC):
        product_gradient(n)
    gather_pass(1, 3)
    gather_pass(3, 3)
    share_end()
    weight_rows(0)
    weight_rows(2)
    mixed_end()
    filters_end()
    weight_rows(1)
    weight_rows(3)

    for copy in sends:
        copy.wait_send()

    def sent(d, carry):
        remote(rg.at[0], rg.at[0], S_LG + d, s, sib).wait_send()
        remote(fg.at[rows_of(s), :], fg.at[rows_of(s), :], S_FG + d, s, sib).wait_send()
        return carry

    lax.fori_loop(1, NCTX, sent, 0)
    lax.fori_loop(0, 16, spread_sent, 0)


def write_out(*refs):
    sources, targets, done = refs[:6], refs[6:12], refs[12]
    copies = [pltpu.make_async_copy(a, b, done.at[n]) for n, (a, b) in enumerate(zip(sources, targets))]
    for copy in copies:
        copy.start()
    for copy in copies:
        copy.wait()


def per_device(forward, inverse, query_proj, key_proj, value_proj, filters, out_weight, cotangent):
    sds = jax.ShapeDtypeStruct
    tile = (TOK, CH)
    V = pltpu.VMEM
    anywhere = pl.BlockSpec(memory_space=pltpu.HBM)
    scratch = [
        V(tile, BF), V(tile, BF), V(tile, BF), V((CH, TAPS), BF), V((CH, NCHAN * CH), BF),
        V((NCHAN,) + tile, BF), V((2, N, N), BF), V((2, N, N), BF),
        V((N, CH), BF), V((N, CH), F32), V((N, CH), F32), V((N, CH), F32), V(tile, F32), V(tile, BF),
        V((NCTX, CH, TOK), BF), V((NCTX, TOK, COLS), BF),
        V((4,) + tile, BF), V((4,) + tile, F32), V((4,) + tile, BF), V((6, 64, CH), BF), V((6, 64, CH), BF),
        V(tile, F32), V(tile, BF), V(tile, BF), V((CH, TAPS), BF), V((NCTX, 64, TAPS), BF),
        V((CH, TAPS), BF),
        pltpu.SemaphoreType.DMA((8,)), pltpu.SemaphoreType.DMA((4,)),
        pltpu.SemaphoreType.DMA((N_SEMS,)), pltpu.SemaphoreType.DMA((N_SEMS,)),
    ]
    shapes = [(tile, BF)] * 4 + [((CH, TAPS), F32), ((CH, COLS), BF)]
    inside = pl.BlockSpec(memory_space=pltpu.VMEM)
    results = pl.pallas_call(
        kernel,
        out_shape=tuple(V(shape, dtype) for shape, dtype in shapes),
        in_specs=[anywhere] * 8,
        out_specs=(inside,) * 6,
        scratch_shapes=scratch,
        compiler_params=pltpu.CompilerParams(
            collective_id=0, has_side_effects=True, vmem_limit_bytes=61 * 2**20),
        cost_estimate=pl.CostEstimate(
            flops=7_000_000_000, bytes_accessed=24_000_000, transcendentals=0),
    )(query_proj, key_proj, value_proj, filters, out_weight, cotangent, forward, inverse)
    return pl.pallas_call(
        write_out,
        out_shape=tuple(sds(shape, dtype) for shape, dtype in shapes),
        in_specs=[inside] * 6,
        out_specs=(anywhere,) * 6,
        scratch_shapes=[pltpu.SemaphoreType.DMA((6,))],
        compiler_params=pltpu.CompilerParams(vmem_limit_bytes=4 * 2**20),
    )(*results)


def solution(mesh):
    forward, inverse = transforms()
    placed = (
        P("ctx", "chan"), P("ctx", "chan"), P("ctx", "chan"),
        P("chan", None), P("chan", None), P("ctx", "chan"),
    )

    def body(*args):
        return per_device(jnp.asarray(forward), jnp.asarray(inverse), *args)

    return jax.shard_map(
        body,
        mesh=mesh,
        in_specs=placed,
        out_specs=(
            P("ctx", "chan"), P("ctx", "chan"), P("ctx", "chan"), P("ctx", "chan"),
            P("chan", None), P("chan", "ctx"),
        ),
        check_vma=False,
    )
```

```python
import functools

import jax
import jax.numpy as jnp
import numpy as np
from jax import lax
from jax.experimental import pallas as pl
from jax.experimental.pallas import tpu as pltpu
from jax.sharding import PartitionSpec as P

MESH = pl.DeviceIdType.MESH
BF = jnp.bfloat16
F32 = jnp.float32

TOK = 128
CH = 1024
TAPS = 128
N = 256
NCTX = 16
NCHAN = 8
COLS = 512
CC_W = 256
NC = CH // CC_W
SPANS = ((0, 256), (512, 256), (256, 256), (768, 256))
ORDER = (0, 2, 1, 3)


def transforms():
    k = np.arange(128, dtype=np.float64)[:, None] + 0.5
    n = np.arange(N, dtype=np.float64)[None, :]
    angle = 2.0 * np.pi * k * n / N
    forward = np.concatenate([np.cos(angle), -np.sin(angle)], axis=0)
    inverse = forward.T / 128.0

    def split(m):
        high = m.astype(jnp.bfloat16)
        low = (m - high.astype(np.float64)).astype(jnp.bfloat16)
        return np.stack([high, low])

    return split(forward), split(inverse)


class Sems:
    def __init__(self):
        self.count = 0

    def take(self, n):
        base = self.count
        self.count += n
        return base


LAYOUT = Sems()
S_HALO = LAYOUT.take(NC)
S_COT = LAYOUT.take(4)
S_COTS = LAYOUT.take(4)
S_A2A = LAYOUT.take(16)
S_X3 = LAYOUT.take(4)
S_X3S = LAYOUT.take(4)
S_AG = LAYOUT.take(NC * 20)
S_MS = LAYOUT.take(4)
S_RS = LAYOUT.take(6)
S_GH = LAYOUT.take(NC)
S_LG = LAYOUT.take(16)
S_FG = LAYOUT.take(16)
N_SEMS = LAYOUT.count


def dot(a, b):
    return jnp.dot(a, b, preferred_element_type=F32)


def dot_nt(a, b):
    return lax.dot_general(a, b, (((1,), (1,)), ((), ())), preferred_element_type=F32)


def kernel(q_in, k_in, v_in, f_in, w_in, cot_in, ef_in, ei_in,
           mixed_b, gq_b, gk_b, gv_b, fgo, gw_b,
           q, k, v, f, w, cot, ef, ei,
           pext, phat, fhat, ghat, filt, gated, gt, cc,
           part, mself, msib, rsend, rrecv, gg, gfb, gnext, lg, rg, fg,
           ld, wl, ss, rs):
    s = lax.axis_index("ctx")
    i = lax.axis_index("chan")
    z, y = s // 4, lax.rem(s, 4)
    x, c = i // 2, lax.rem(i, 2)
    sib = x * 2 + (1 - c)

    def ctx_at(dz, dy):
        return lax.rem(z + dz, 4) * 4 + lax.rem(y + dy, 4)

    def chan_at(dx):
        return lax.rem(x + dx, 4) * 2 + c

    barrier = pltpu.get_barrier_semaphore()

    def greet(d, carry):
        pl.semaphore_signal(barrier, inc=1, device_id=(lax.rem(s + d, NCTX), i), device_id_type=MESH)
        return carry

    for dx in (1, 3):
        pl.semaphore_signal(barrier, inc=1, device_id=(s, chan_at(dx)), device_id_type=MESH)
    pl.semaphore_signal(barrier, inc=1, device_id=(s, sib), device_id_type=MESH)
    lax.fori_loop(1, NCTX, greet, 0)

    def greet_source(d, carry):
        @pl.when(jnp.logical_or(d != s, s // 2 != i))
        def _():
            pl.semaphore_signal(barrier, inc=1, device_id=(d, s // 2), device_id_type=MESH)

        return carry

    lax.fori_loop(0, NCTX, greet_source, 0)

    loads = {}

    def load(name, src, dst, slot):
        loads[name] = pltpu.make_async_copy(src, dst, ld.at[slot])
        loads[name].start()

    load("k", k_in, k, 0)
    load("v", v_in, v, 1)
    load("ef", ef_in, ef, 2)
    load("f", f_in, f, 3)
    load("ei", ei_in, ei, 4)
    load("q", q_in, q, 5)
    load("cot", cot_in, cot.at[i], 6)
    w_loads = []
    for d in range(4):
        columns = pl.ds(d * 2048, 2048)
        copy = pltpu.make_async_copy(w_in.at[:, columns], w.at[:, columns], wl.at[d])
        copy.start()
        w_loads.append(copy)

    def remote(src, dst, slot, ctx, chan):
        return pltpu.make_async_remote_copy(
            src_ref=src, dst_ref=dst, send_sem=ss.at[slot], recv_sem=rs.at[slot],
            device_id=(ctx, chan), device_id_type=MESH)

    sends = []

    def send(src, dst, slot, ctx, chan):
        copy = remote(src, dst, slot, ctx, chan)
        copy.start()
        sends.append(copy)

    def arrived(dst, slot):
        remote(dst, dst, slot, s, sib).wait_recv()

    loads["k"].wait()
    loads["v"].wait()
    pext[pl.ds(TOK, TOK), :] = (k[...].astype(F32) * v[...].astype(F32)).astype(BF)
    loads["cot"].wait()

    pl.semaphore_wait(barrier, NCTX - 1 + 3 + jnp.where(s // 2 == i, 15, 16))

    after, before = lax.rem(s + 1, NCTX), lax.rem(s + NCTX - 1, NCTX)
    for n in ORDER:
        columns = pl.ds(*SPANS[n])
        send(pext.at[pl.ds(TOK, TOK), columns], pext.at[pl.ds(0, TOK), columns], S_HALO + n, after, i)
    mine = pl.ds(pl.multiple_of(i * 16, 16), 16)

    def spread_copy(d):
        target, chan = 2 * i + d // NCHAN, lax.rem(d, NCHAN)
        rows = pl.ds(pl.multiple_of(chan * 16, 16), 16)
        columns = pl.ds(pl.multiple_of((d // NCHAN) * COLS, COLS), COLS)
        return target, chan, pltpu.make_async_remote_copy(
            src_ref=cot.at[i, rows, columns], dst_ref=cc.at[s, rows, :],
            send_sem=ss.at[S_A2A + d], recv_sem=rs.at[S_A2A + s],
            device_id=(target, chan), device_id_type=MESH)

    def spread(d, carry):
        target, chan, copy = spread_copy(d)

        @pl.when(jnp.logical_or(target != s, chan != i))
        def _():
            copy.start()

        return carry

    def spread_sent(d, carry):
        target, chan, copy = spread_copy(d)

        @pl.when(jnp.logical_or(target != s, chan != i))
        def _():
            copy.wait_send()

        return carry

    def spread_done(b, carry):
        @pl.when(jnp.logical_or(b != s, s // 2 != i))
        def _():
            remote(cc.at[b, mine, :], cc.at[b, mine, :], S_A2A + b, s, sib).wait_recv()

        return carry

    lax.fori_loop(0, 16, spread, 0)

    @pl.when(s // 2 == i)
    def _():
        cc[s, mine, :] = cot[i, mine, pl.ds(pl.multiple_of(lax.rem(s, 2) * COLS, COLS), COLS)]

    for m, dx in enumerate((1, 3)):
        send(cot.at[i], cot.at[i], S_COT + m, s, chan_at(dx))
    send(cot.at[i], cot.at[i], S_COTS, s, sib)

    loads["ef"].wait()
    loads["f"].wait()
    for n in range(NC):
        taps = f[pl.ds(n * CC_W, CC_W), :]
        fhat[:, pl.ds(n * CC_W, CC_W)] = dot_nt(ef[0, :, 0:TOK], taps) + dot_nt(ef[1, :, 0:TOK], taps)
    loads["ei"].wait()
    loads["q"].wait()
    has_before = jnp.where(s > 0, 1.0, 0.0).astype(BF)
    has_after = jnp.where(s < NCTX - 1, 1.0, 0.0).astype(BF)

    def inverse(rows, spectrum):
        high = spectrum.astype(BF)
        low = (spectrum - high.astype(F32)).astype(BF)
        return dot(ei[0, rows, :], high) + (dot(ei[0, rows, :], low) + dot(ei[1, rows, :], high))

    lower, upper = slice(0, TOK), slice(TOK, N)

    def at(n, da, db):
        return ctx_at(db, da) if n < 2 else ctx_at(da, db)

    def gated_send(n, da, db, half, slot, to_a, to_b):
        start, size = SPANS[n]
        rows = pl.ds(start, size) if half is None else pl.ds(start + half * (size // 2), size // 2)
        block = gt.at[at(n, da, db), rows, :]
        send(block, block, S_AG + n * 20 + slot, at(n, to_a, to_b), i)

    def gated_wait(n, da, db, half, slot):
        start, size = SPANS[n]
        rows = pl.ds(start, size) if half is None else pl.ds(start + half * (size // 2), size // 2)
        arrived(gt.at[at(n, da, db), rows, :], S_AG + n * 20 + slot)

    def along_second(n, t, da):
        gated_send(n, da, 0, None, 4 + 4 * t, 0, 1)
        gated_send(n, da, 0, None, 5 + 4 * t, 0, 3)

    def gather_own(n):
        gated_send(n, 0, 0, None, 0, 1, 0)
        gated_send(n, 0, 0, None, 1, 3, 0)
        along_second(n, 0, 0)

    def gather_near(n):
        gated_wait(n, 3, 0, None, 0)
        gated_send(n, 3, 0, 0, 2, 1, 0)
        along_second(n, 1, 3)
        gated_wait(n, 1, 0, None, 1)
        gated_send(n, 1, 0, 1, 3, 3, 0)
        along_second(n, 2, 1)

    def gather_far(n):
        gated_wait(n, 2, 0, 0, 2)
        gated_wait(n, 2, 0, 1, 3)
        along_second(n, 3, 2)

    offset_of = (0, 3, 1, 2)

    def gather_pass(n, t):
        da = offset_of[t]
        gated_wait(n, da, 3, None, 4 + 4 * t)
        gated_send(n, da, 3, 0, 6 + 4 * t, 0, 1)
        gated_wait(n, da, 1, None, 5 + 4 * t)
        gated_send(n, da, 1, 1, 7 + 4 * t, 0, 3)

    def gather_end(n, t):
        da = offset_of[t]
        gated_wait(n, da, 2, 0, 6 + 4 * t)
        gated_wait(n, da, 2, 1, 7 + 4 * t)

    def x_near(view, slot, sib_slot):
        for m, (source, target) in enumerate(((3, 1), (1, 3))):
            block = chan_at(source)
            arrived(view(block), slot + m)
            send(view(block, m), view(block, m), slot + 2 + m, s, chan_at(target))
            send(view(block), view(block), sib_slot + 1 + m, s, sib)

    def x_far(view, slot, sib_slot):
        block = chan_at(2)
        for m in range(2):
            arrived(view(block, m), slot + 2 + m)
        send(view(block), view(block), sib_slot + 3, s, sib)

    def cot_view(block, half=None):
        return cot.at[block] if half is None else cot.at[block, pl.ds(half * 64, 64), :]

    def share(block, half=None):
        rows = pl.ds(pl.multiple_of(block * 16, 16), 16)
        return cc.at[:, rows, :] if half is None else cc.at[pl.ds(half * 8, 8), rows, :]

    def mixed_part(dx):
        chip = lax.rem(x + dx, 4)
        both = dot(gated[...], w[:, pl.ds(pl.multiple_of(chip * 2 * CH, 2 * CH), 2 * CH)])
        first, second = both[:, :CH], both[:, CH:]
        part[dx] = jnp.where(c == 0, second, first).astype(BF)
        send(part.at[dx], msib.at[dx], S_MS + dx, s, sib)
        mself[dx] = jnp.where(c == 0, first, second)

    top, bottom = pl.ds(0, 64), pl.ds(64, 64)

    def chip_sum(dx, rows):
        return mself[dx, rows, :] + msib[dx, rows, :].astype(F32)

    def mixed_send(m, dx, value):
        rsend[m] = value.astype(BF)
        send(rsend.at[m], rrecv.at[m], S_RS + m, s, chan_at(dx))

    def mixed_far():
        arrived(msib.at[2], S_MS + 2)
        mixed_send(0, 1, chip_sum(2, top))
        mixed_send(1, 3, chip_sum(2, bottom))

    def mixed_near():
        arrived(msib.at[1], S_MS + 1)
        mixed_send(2, 1, chip_sum(1, bottom))
        arrived(msib.at[3], S_MS + 3)
        mixed_send(3, 3, chip_sum(3, top))

    def mixed_last():
        arrived(rrecv.at[0], S_RS)
        mixed_send(4, 1, chip_sum(1, top) + rrecv[0].astype(F32))
        arrived(rrecv.at[1], S_RS + 1)
        mixed_send(5, 3, chip_sum(3, bottom) + rrecv[1].astype(F32))

    def mixed_end():
        arrived(msib.at[0], S_MS)
        for m in (2, 3, 4, 5):
            arrived(rrecv.at[m], S_RS + m)
        mixed_b[top, :] = (chip_sum(0, top) + rrecv[4].astype(F32) + rrecv[3].astype(F32)).astype(BF)
        mixed_b[bottom, :] = (chip_sum(0, bottom) + rrecv[2].astype(F32) + rrecv[5].astype(F32)).astype(BF)

    def gated_chunk(n):
        columns = pl.ds(*SPANS[n])
        arrived(pext.at[pl.ds(0, TOK), columns], S_HALO + n)
        halo = pext[pl.ds(0, TOK), columns] * has_before
        both = jnp.concatenate([halo, pext[pl.ds(TOK, TOK), columns]], axis=0)
        spectrum = dot(ef[0], both) + dot(ef[1], both)
        phat[:, columns] = spectrum
        taps = fhat[:, columns]
        pr, pi, fr, fi = spectrum[:128], spectrum[128:], taps[:128], taps[128:]
        filtered = inverse(upper, jnp.concatenate([pr * fr - pi * fi, pr * fi + pi * fr], axis=0))
        filt[:, columns] = filtered
        value = q[:, columns].astype(F32) * filtered
        gated[:, columns] = value.astype(BF)
        gt[s, columns, :] = value.T.astype(BF)

    def share_out():
        lax.fori_loop(0, NCTX, spread_done, 0)
        for m, dx in enumerate((1, 3)):
            send(share(i), share(i), S_X3 + m, s, chan_at(dx))
        send(share(i), share(i), S_X3S, s, sib)

    def grad_gated_part(dx, slot):
        chip = lax.rem(x + dx, 4)
        arrived(cot.at[chip * 2 + (1 - c)], S_COTS + slot)
        row = jnp.concatenate([cot[chip * 2], cot[chip * 2 + 1]], axis=1)
        term = dot_nt(row, w[:, pl.ds(pl.multiple_of(chip * 2 * CH, 2 * CH), 2 * CH)])
        if slot == 0:
            gg[...] = term
        else:
            gg[...] += term

    def gradients():
        grad = gg[...]
        gfb[...] = (grad * q[...].astype(F32)).astype(BF)
        for n in range(NC):
            columns = pl.ds(n * CC_W, CC_W)
            send(gfb.at[:, columns], gnext.at[:, columns], S_GH + n, before, i)
        gq_b[...] = (grad * filt[...]).astype(BF)

    def filter_terms(n):
        columns = pl.ds(n * CC_W, CC_W)
        block = gfb[:, columns]
        g = dot(ef[0, :, 0:TOK], block) + dot(ef[1, :, 0:TOK], block)
        ghat[:, columns] = g
        p = phat[:, columns]
        pr, pi, gr, gi = p[:128], p[128:], g[:128], g[128:]
        taps = inverse(upper, jnp.concatenate([gr * pr + gi * pi, gi * pr - gr * pi], axis=0))
        lg[columns, :] = (-taps).T.astype(BF)

    def rows_of(target):
        return pl.ds(pl.multiple_of(target * 64, 64), 64)

    def scatter(d, carry):
        target = lax.rem(s + d, NCTX)
        remote(lg.at[rows_of(target), :], rg.at[s], S_LG + d, target, i).start()
        return carry

    def scatter_done(d, carry):
        source = lax.rem(s + NCTX - d, NCTX)
        remote(rg.at[source], rg.at[source], S_LG + d, s, sib).wait_recv()
        return carry

    def publish(d, carry):
        remote(fg.at[rows_of(s), :], fg.at[rows_of(s), :], S_FG + d, lax.rem(s + d, NCTX), i).start()
        return carry

    def publish_done(d, carry):
        rows = rows_of(lax.rem(s + NCTX - d, NCTX))
        remote(fg.at[rows, :], fg.at[rows, :], S_FG + d, s, sib).wait_recv()
        return carry

    def filters_out():
        lax.fori_loop(1, NCTX, scatter, 0)
        rg[s] = lg[rows_of(s), :]

    def filters_sum():
        lax.fori_loop(1, NCTX, scatter_done, 0)
        total = rg[0].astype(F32)
        for b in range(1, NCTX):
            total = total + rg[b].astype(F32)
        fg[rows_of(s), :] = total.astype(BF)
        lax.fori_loop(1, NCTX, publish, 0)

    def filters_end():
        lax.fori_loop(1, NCTX, publish_done, 0)
        fgo[...] = fg[...].astype(F32)

    def product_gradient(n):
        columns = pl.ds(n * CC_W, CC_W)
        arrived(gnext.at[:, columns], S_GH + n)
        block = gnext[:, columns] * has_after
        g = ghat[:, columns] + (dot(ef[0, :, TOK:N], block) + dot(ef[1, :, TOK:N], block))
        taps = fhat[:, columns]
        gr, gi, fr, fi = g[:128], g[128:], taps[:128], taps[128:]
        grad_product = inverse(lower, jnp.concatenate([gr * fr + gi * fi, gi * fr - gr * fi], axis=0))
        gk_b[:, columns] = (grad_product * v[:, columns].astype(F32)).astype(BF)
        gv_b[:, columns] = (grad_product * k[:, columns].astype(F32)).astype(BF)

    def share_end():
        for slot, dx in enumerate((0, 3, 1, 2)):
            arrived(share(lax.rem(x + dx, 4) * 2 + (1 - c)), S_X3S + slot)

    def weight_rows(n):
        for t in range(4):
            gather_end(n, t)
        rows = pl.ds(*SPANS[n])
        left = jnp.concatenate([gt[b, rows, :] for b in range(NCTX)], axis=1)
        gw_b[rows, :] = dot(left, cc[...].reshape(NCTX * TOK, COLS)).astype(BF)

    for copy in w_loads:
        copy.wait()
    grad_gated_part(0, 0)
    gated_chunk(0)
    gather_own(0)
    gated_chunk(2)
    gather_own(2)
    gated_chunk(1)
    gather_own(1)
    gated_chunk(3)
    gather_own(3)
    x_near(cot_view, S_COT, S_COTS)
    share_out()
    gather_near(0)
    gather_near(2)
    grad_gated_part(3, 1)
    gather_pass(0, 0)
    gather_pass(2, 0)
    gather_near(1)
    gather_near(3)
    x_far(cot_view, S_COT, S_COTS)
    grad_gated_part(1, 2)
    gather_pass(1, 0)
    gather_pass(3, 0)
    gather_far(0)
    gather_far(2)
    grad_gated_part(2, 3)
    x_near(share, S_X3, S_X3S)
    gradients()
    gather_pass(0, 1)
    gather_pass(2, 1)
    gather_pass(1, 1)
    gather_pass(3, 1)
    filter_terms(0)
    filter_terms(1)
    filter_terms(2)
    filter_terms(3)
    filters_out()
    gather_far(1)
    gather_far(3)
    mixed_part(2)
    gather_pass(0, 2)
    gather_pass(2, 2)
    mixed_far()
    mixed_part(1)
    gather_pass(1, 2)
    gather_pass(3, 2)
    mixed_part(3)
    mixed_near()
    x_far(share, S_X3, S_X3S)
    gather_pass(0, 3)
    gather_pass(2, 3)
    mixed_part(0)
    mixed_last()
    gather_pass(1, 3)
    gather_pass(3, 3)
    filters_sum()
    product_gradient(0)
    product_gradient(1)
    product_gradient(2)
    product_gradient(3)
    share_end()
    weight_rows(0)
    weight_rows(2)
    mixed_end()
    weight_rows(1)
    weight_rows(3)
    filters_end()

    for copy in sends:
        copy.wait_send()

    def sent(d, carry):
        remote(rg.at[0], rg.at[0], S_LG + d, s, sib).wait_send()
        remote(fg.at[rows_of(s), :], fg.at[rows_of(s), :], S_FG + d, s, sib).wait_send()
        return carry

    lax.fori_loop(1, NCTX, sent, 0)
    lax.fori_loop(0, 16, spread_sent, 0)


def write_out(*refs):
    sources, targets, done = refs[:6], refs[6:12], refs[12]
    copies = [pltpu.make_async_copy(a, b, done.at[n]) for n, (a, b) in enumerate(zip(sources, targets))]
    for copy in copies:
        copy.start()
    for copy in copies:
        copy.wait()


def per_device(forward, inverse, query_proj, key_proj, value_proj, filters, out_weight, cotangent):
    sds = jax.ShapeDtypeStruct
    tile = (TOK, CH)
    V = pltpu.VMEM
    anywhere = pl.BlockSpec(memory_space=pltpu.HBM)
    scratch = [
        V(tile, BF), V(tile, BF), V(tile, BF), V((CH, TAPS), BF), V((CH, NCHAN * CH), BF),
        V((NCHAN,) + tile, BF), V((2, N, N), BF), V((2, N, N), BF),
        V((N, CH), BF), V((N, CH), F32), V((N, CH), F32), V((N, CH), F32), V(tile, F32), V(tile, BF),
        V((NCTX, CH, TOK), BF), V((NCTX, TOK, COLS), BF),
        V((4,) + tile, BF), V((4,) + tile, F32), V((4,) + tile, BF), V((6, 64, CH), BF), V((6, 64, CH), BF),
        V(tile, F32), V(tile, BF), V(tile, BF), V((CH, TAPS), BF), V((NCTX, 64, TAPS), BF),
        V((CH, TAPS), BF),
        pltpu.SemaphoreType.DMA((8,)), pltpu.SemaphoreType.DMA((4,)),
        pltpu.SemaphoreType.DMA((N_SEMS,)), pltpu.SemaphoreType.DMA((N_SEMS,)),
    ]
    shapes = [(tile, BF)] * 4 + [((CH, TAPS), F32), ((CH, COLS), BF)]
    inside = pl.BlockSpec(memory_space=pltpu.VMEM)
    results = pl.pallas_call(
        kernel,
        out_shape=tuple(V(shape, dtype) for shape, dtype in shapes),
        in_specs=[anywhere] * 8,
        out_specs=(inside,) * 6,
        scratch_shapes=scratch,
        compiler_params=pltpu.CompilerParams(
            collective_id=0, has_side_effects=True, vmem_limit_bytes=61 * 2**20),
        cost_estimate=pl.CostEstimate(
            flops=7_000_000_000, bytes_accessed=24_000_000, transcendentals=0),
    )(query_proj, key_proj, value_proj, filters, out_weight, cotangent, forward, inverse)
    return pl.pallas_call(
        write_out,
        out_shape=tuple(sds(shape, dtype) for shape, dtype in shapes),
        in_specs=[inside] * 6,
        out_specs=(anywhere,) * 6,
        scratch_shapes=[pltpu.SemaphoreType.DMA((6,))],
        compiler_params=pltpu.CompilerParams(vmem_limit_bytes=4 * 2**20),
    )(*results)


def solution(mesh):
    forward, inverse = transforms()
    placed = (
        P("ctx", "chan"), P("ctx", "chan"), P("ctx", "chan"),
        P("chan", None), P("chan", None), P("ctx", "chan"),
    )

    def body(*args):
        return per_device(jnp.asarray(forward), jnp.asarray(inverse), *args)

    return jax.shard_map(
        body,
        mesh=mesh,
        in_specs=placed,
        out_specs=(
            P("ctx", "chan"), P("ctx", "chan"), P("ctx", "chan"), P("ctx", "chan"),
            P("chan", None), P("chan", "ctx"),
        ),
        check_vma=False,
    )
```

```python
import functools

import jax
import jax.numpy as jnp
import numpy as np
from jax import lax
from jax.experimental import pallas as pl
from jax.experimental.pallas import tpu as pltpu
from jax.sharding import PartitionSpec as P

MESH = pl.DeviceIdType.MESH
BF = jnp.bfloat16
F32 = jnp.float32

TOK = 128
CH = 1024
TAPS = 128
N = 256
NCTX = 16
NCHAN = 8
COLS = 512
CC_W = 256
NC = CH // CC_W
SPANS = ((0, 256), (512, 256), (256, 256), (768, 256))
ORDER = (0, 2, 1, 3)


def transforms():
    k = np.arange(128, dtype=np.float64)[:, None] + 0.5
    n = np.arange(N, dtype=np.float64)[None, :]
    angle = 2.0 * np.pi * k * n / N
    forward = np.concatenate([np.cos(angle), -np.sin(angle)], axis=0)
    inverse = forward.T / 128.0

    def split(m):
        high = m.astype(jnp.bfloat16)
        low = (m - high.astype(np.float64)).astype(jnp.bfloat16)
        return np.stack([high, low])

    return split(forward), split(inverse)


class Sems:
    def __init__(self):
        self.count = 0

    def take(self, n):
        base = self.count
        self.count += n
        return base


LAYOUT = Sems()
S_HALO = LAYOUT.take(NC)
S_COT = LAYOUT.take(4)
S_COTS = LAYOUT.take(4)
S_A2A = LAYOUT.take(16)
S_X3 = LAYOUT.take(4)
S_X3S = LAYOUT.take(4)
S_AG = LAYOUT.take(NC * 20)
S_MS = LAYOUT.take(4)
S_RS = LAYOUT.take(6)
S_GH = LAYOUT.take(NC)
S_LG = LAYOUT.take(16)
S_FG = LAYOUT.take(16)
N_SEMS = LAYOUT.count


def dot(a, b):
    return jnp.dot(a, b, preferred_element_type=F32)


def dot_nt(a, b):
    return lax.dot_general(a, b, (((1,), (1,)), ((), ())), preferred_element_type=F32)


def kernel(q_in, k_in, v_in, f_in, w_in, cot_in, ef_in, ei_in,
           mixed_b, gq_b, gk_b, gv_b, fgo, gw_b,
           q, k, v, f, w, cot, ef, ei,
           pext, phat, fhat, ghat, filt, gated, gt, cc,
           part, mself, msib, rsend, rrecv, gg, gfb, gnext, lg, rg, fg,
           ld, wl, ss, rs):
    s = lax.axis_index("ctx")
    i = lax.axis_index("chan")
    z, y = s // 4, lax.rem(s, 4)
    x, c = i // 2, lax.rem(i, 2)
    sib = x * 2 + (1 - c)

    def ctx_at(dz, dy):
        return lax.rem(z + dz, 4) * 4 + lax.rem(y + dy, 4)

    def chan_at(dx):
        return lax.rem(x + dx, 4) * 2 + c

    barrier = pltpu.get_barrier_semaphore()

    def greet(d, carry):
        pl.semaphore_signal(barrier, inc=1, device_id=(lax.rem(s + d, NCTX), i), device_id_type=MESH)
        return carry

    for dx in (1, 3):
        pl.semaphore_signal(barrier, inc=1, device_id=(s, chan_at(dx)), device_id_type=MESH)
    pl.semaphore_signal(barrier, inc=1, device_id=(s, sib), device_id_type=MESH)
    lax.fori_loop(1, NCTX, greet, 0)

    def greet_source(d, carry):
        @pl.when(jnp.logical_or(d != s, s // 2 != i))
        def _():
            pl.semaphore_signal(barrier, inc=1, device_id=(d, s // 2), device_id_type=MESH)

        return carry

    lax.fori_loop(0, NCTX, greet_source, 0)

    loads = {}

    def load(name, src, dst, slot):
        loads[name] = pltpu.make_async_copy(src, dst, ld.at[slot])
        loads[name].start()

    load("k", k_in, k, 0)
    load("v", v_in, v, 1)
    load("ef", ef_in, ef, 2)
    load("f", f_in, f, 3)
    load("ei", ei_in, ei, 4)
    load("q", q_in, q, 5)
    load("cot", cot_in, cot.at[i], 6)
    w_loads = []
    for d in range(4):
        columns = pl.ds(d * 2048, 2048)
        copy = pltpu.make_async_copy(w_in.at[:, columns], w.at[:, columns], wl.at[d])
        copy.start()
        w_loads.append(copy)

    def remote(src, dst, slot, ctx, chan):
        return pltpu.make_async_remote_copy(
            src_ref=src, dst_ref=dst, send_sem=ss.at[slot], recv_sem=rs.at[slot],
            device_id=(ctx, chan), device_id_type=MESH)

    sends = []

    def send(src, dst, slot, ctx, chan):
        copy = remote(src, dst, slot, ctx, chan)
        copy.start()
        sends.append(copy)

    def arrived(dst, slot):
        remote(dst, dst, slot, s, sib).wait_recv()

    loads["k"].wait()
    loads["v"].wait()
    pext[pl.ds(TOK, TOK), :] = (k[...].astype(F32) * v[...].astype(F32)).astype(BF)
    loads["cot"].wait()

    pl.semaphore_wait(barrier, NCTX - 1 + 3 + jnp.where(s // 2 == i, 15, 16))

    after, before = lax.rem(s + 1, NCTX), lax.rem(s + NCTX - 1, NCTX)
    for n in ORDER:
        columns = pl.ds(*SPANS[n])
        send(pext.at[pl.ds(TOK, TOK), columns], pext.at[pl.ds(0, TOK), columns], S_HALO + n, after, i)
    mine = pl.ds(pl.multiple_of(i * 16, 16), 16)

    def spread_copy(d):
        target, chan = 2 * i + d // NCHAN, lax.rem(d, NCHAN)
        rows = pl.ds(pl.multiple_of(chan * 16, 16), 16)
        columns = pl.ds(pl.multiple_of((d // NCHAN) * COLS, COLS), COLS)
        return target, chan, pltpu.make_async_remote_copy(
            src_ref=cot.at[i, rows, columns], dst_ref=cc.at[s, rows, :],
            send_sem=ss.at[S_A2A + d], recv_sem=rs.at[S_A2A + s],
            device_id=(target, chan), device_id_type=MESH)

    def spread(d, carry):
        target, chan, copy = spread_copy(d)

        @pl.when(jnp.logical_or(target != s, chan != i))
        def _():
            copy.start()

        return carry

    def spread_sent(d, carry):
        target, chan, copy = spread_copy(d)

        @pl.when(jnp.logical_or(target != s, chan != i))
        def _():
            copy.wait_send()

        return carry

    def spread_done(b, carry):
        @pl.when(jnp.logical_or(b != s, s // 2 != i))
        def _():
            remote(cc.at[b, mine, :], cc.at[b, mine, :], S_A2A + b, s, sib).wait_recv()

        return carry

    lax.fori_loop(0, 16, spread, 0)

    @pl.when(s // 2 == i)
    def _():
        cc[s, mine, :] = cot[i, mine, pl.ds(pl.multiple_of(lax.rem(s, 2) * COLS, COLS), COLS)]

    for m, dx in enumerate((1, 3)):
        send(cot.at[i], cot.at[i], S_COT + m, s, chan_at(dx))
    send(cot.at[i], cot.at[i], S_COTS, s, sib)

    loads["ef"].wait()
    loads["f"].wait()
    for n in range(NC):
        taps = f[pl.ds(n * CC_W, CC_W), :]
        fhat[:, pl.ds(n * CC_W, CC_W)] = dot_nt(ef[0, :, 0:TOK], taps) + dot_nt(ef[1, :, 0:TOK], taps)
    loads["ei"].wait()
    loads["q"].wait()
    has_before = jnp.where(s > 0, 1.0, 0.0).astype(BF)
    has_after = jnp.where(s < NCTX - 1, 1.0, 0.0).astype(BF)

    def inverse(rows, spectrum):
        high = spectrum.astype(BF)
        low = (spectrum - high.astype(F32)).astype(BF)
        return dot(ei[0, rows, :], high) + (dot(ei[0, rows, :], low) + dot(ei[1, rows, :], high))

    lower, upper = slice(0, TOK), slice(TOK, N)

    def at(n, da, db):
        return ctx_at(db, da) if n < 2 else ctx_at(da, db)

    def gated_send(n, da, db, half, slot, to_a, to_b):
        start, size = SPANS[n]
        rows = pl.ds(start, size) if half is None else pl.ds(start + half * (size // 2), size // 2)
        block = gt.at[at(n, da, db), rows, :]
        send(block, block, S_AG + n * 20 + slot, at(n, to_a, to_b), i)

    def gated_wait(n, da, db, half, slot):
        start, size = SPANS[n]
        rows = pl.ds(start, size) if half is None else pl.ds(start + half * (size // 2), size // 2)
        arrived(gt.at[at(n, da, db), rows, :], S_AG + n * 20 + slot)

    def along_second(n, t, da):
        gated_send(n, da, 0, None, 4 + 4 * t, 0, 1)
        gated_send(n, da, 0, None, 5 + 4 * t, 0, 3)

    def gather_own(n):
        gated_send(n, 0, 0, None, 0, 1, 0)
        gated_send(n, 0, 0, None, 1, 3, 0)
        along_second(n, 0, 0)

    def gather_near(n):
        gated_wait(n, 3, 0, None, 0)
        gated_send(n, 3, 0, 0, 2, 1, 0)
        along_second(n, 1, 3)
        gated_wait(n, 1, 0, None, 1)
        gated_send(n, 1, 0, 1, 3, 3, 0)
        along_second(n, 2, 1)

    def gather_far(n):
        gated_wait(n, 2, 0, 0, 2)
        gated_wait(n, 2, 0, 1, 3)
        along_second(n, 3, 2)

    offset_of = (0, 3, 1, 2)

    def gather_pass(n, t):
        da = offset_of[t]
        gated_wait(n, da, 3, None, 4 + 4 * t)
        gated_send(n, da, 3, 0, 6 + 4 * t, 0, 1)
        gated_wait(n, da, 1, None, 5 + 4 * t)
        gated_send(n, da, 1, 1, 7 + 4 * t, 0, 3)

    def gather_end(n, t):
        da = offset_of[t]
        gated_wait(n, da, 2, 0, 6 + 4 * t)
        gated_wait(n, da, 2, 1, 7 + 4 * t)

    def x_near(view, slot, sib_slot):
        for m, (source, target) in enumerate(((3, 1), (1, 3))):
            block = chan_at(source)
            arrived(view(block), slot + m)
            send(view(block, m), view(block, m), slot + 2 + m, s, chan_at(target))
            send(view(block), view(block), sib_slot + 1 + m, s, sib)

    def x_far(view, slot, sib_slot):
        block = chan_at(2)
        for m in range(2):
            arrived(view(block, m), slot + 2 + m)
        send(view(block), view(block), sib_slot + 3, s, sib)

    def cot_view(block, half=None):
        return cot.at[block] if half is None else cot.at[block, pl.ds(half * 64, 64), :]

    def share(block, half=None):
        rows = pl.ds(pl.multiple_of(block * 16, 16), 16)
        return cc.at[:, rows, :] if half is None else cc.at[pl.ds(half * 8, 8), rows, :]

    def mixed_part(dx):
        chip = lax.rem(x + dx, 4)
        both = dot(gated[...], w[:, pl.ds(pl.multiple_of(chip * 2 * CH, 2 * CH), 2 * CH)])
        first, second = both[:, :CH], both[:, CH:]
        part[dx] = jnp.where(c == 0, second, first).astype(BF)
        send(part.at[dx], msib.at[dx], S_MS + dx, s, sib)
        mself[dx] = jnp.where(c == 0, first, second)

    top, bottom = pl.ds(0, 64), pl.ds(64, 64)

    def chip_sum(dx, rows):
        return mself[dx, rows, :] + msib[dx, rows, :].astype(F32)

    def mixed_send(m, dx, value):
        rsend[m] = value.astype(BF)
        send(rsend.at[m], rrecv.at[m], S_RS + m, s, chan_at(dx))

    def mixed_far():
        arrived(msib.at[2], S_MS + 2)
        mixed_send(0, 1, chip_sum(2, top))
        mixed_send(1, 3, chip_sum(2, bottom))

    def mixed_near():
        arrived(msib.at[1], S_MS + 1)
        mixed_send(2, 1, chip_sum(1, bottom))
        arrived(msib.at[3], S_MS + 3)
        mixed_send(3, 3, chip_sum(3, top))

    def mixed_last():
        arrived(rrecv.at[0], S_RS)
        mixed_send(4, 1, chip_sum(1, top) + rrecv[0].astype(F32))
        arrived(rrecv.at[1], S_RS + 1)
        mixed_send(5, 3, chip_sum(3, bottom) + rrecv[1].astype(F32))

    def mixed_end():
        arrived(msib.at[0], S_MS)
        for m in (2, 3, 4, 5):
            arrived(rrecv.at[m], S_RS + m)
        mixed_b[top, :] = (chip_sum(0, top) + rrecv[4].astype(F32) + rrecv[3].astype(F32)).astype(BF)
        mixed_b[bottom, :] = (chip_sum(0, bottom) + rrecv[2].astype(F32) + rrecv[5].astype(F32)).astype(BF)

    def gated_chunk(n):
        columns = pl.ds(*SPANS[n])
        arrived(pext.at[pl.ds(0, TOK), columns], S_HALO + n)
        halo = pext[pl.ds(0, TOK), columns] * has_before
        both = jnp.concatenate([halo, pext[pl.ds(TOK, TOK), columns]], axis=0)
        spectrum = dot(ef[0], both) + dot(ef[1], both)
        phat[:, columns] = spectrum
        taps = fhat[:, columns]
        pr, pi, fr, fi = spectrum[:128], spectrum[128:], taps[:128], taps[128:]
        filtered = inverse(upper, jnp.concatenate([pr * fr - pi * fi, pr * fi + pi * fr], axis=0))
        filt[:, columns] = filtered
        value = q[:, columns].astype(F32) * filtered
        gated[:, columns] = value.astype(BF)
        gt[s, columns, :] = value.T.astype(BF)

    def share_out():
        lax.fori_loop(0, NCTX, spread_done, 0)
        for m, dx in enumerate((1, 3)):
            send(share(i), share(i), S_X3 + m, s, chan_at(dx))
        send(share(i), share(i), S_X3S, s, sib)

    def grad_gated_part(dx, slot):
        chip = lax.rem(x + dx, 4)
        arrived(cot.at[chip * 2 + (1 - c)], S_COTS + slot)
        row = jnp.concatenate([cot[chip * 2], cot[chip * 2 + 1]], axis=1)
        term = dot_nt(row, w[:, pl.ds(pl.multiple_of(chip * 2 * CH, 2 * CH), 2 * CH)])
        if slot == 0:
            gg[...] = term
        else:
            gg[...] += term

    def gradients():
        grad = gg[...]
        gfb[...] = (grad * q[...].astype(F32)).astype(BF)
        for n in range(NC):
            columns = pl.ds(n * CC_W, CC_W)
            send(gfb.at[:, columns], gnext.at[:, columns], S_GH + n, before, i)
        gq_b[...] = (grad * filt[...]).astype(BF)

    def filter_terms(n):
        columns = pl.ds(n * CC_W, CC_W)
        block = gfb[:, columns]
        g = dot(ef[0, :, 0:TOK], block) + dot(ef[1, :, 0:TOK], block)
        ghat[:, columns] = g
        p = phat[:, columns]
        pr, pi, gr, gi = p[:128], p[128:], g[:128], g[128:]
        taps = inverse(upper, jnp.concatenate([gr * pr + gi * pi, gi * pr - gr * pi], axis=0))
        lg[columns, :] = (-taps).T.astype(BF)

    def rows_of(target):
        return pl.ds(pl.multiple_of(target * 64, 64), 64)

    def scatter(d, carry):
        target = lax.rem(s + d, NCTX)
        remote(lg.at[rows_of(target), :], rg.at[s], S_LG + d, target, i).start()
        return carry

    def scatter_done(d, carry):
        source = lax.rem(s + NCTX - d, NCTX)
        remote(rg.at[source], rg.at[source], S_LG + d, s, sib).wait_recv()
        return carry

    def publish(d, carry):
        remote(fg.at[rows_of(s), :], fg.at[rows_of(s), :], S_FG + d, lax.rem(s + d, NCTX), i).start()
        return carry

    def publish_done(d, carry):
        rows = rows_of(lax.rem(s + NCTX - d, NCTX))
        remote(fg.at[rows, :], fg.at[rows, :], S_FG + d, s, sib).wait_recv()
        return carry

    def filters_out():
        lax.fori_loop(1, NCTX, scatter, 0)
        rg[s] = lg[rows_of(s), :]

    def filters_sum():
        lax.fori_loop(1, NCTX, scatter_done, 0)
        total = rg[0].astype(F32)
        for b in range(1, NCTX):
            total = total + rg[b].astype(F32)
        fg[rows_of(s), :] = total.astype(BF)
        lax.fori_loop(1, NCTX, publish, 0)

    def filters_end():
        lax.fori_loop(1, NCTX, publish_done, 0)
        fgo[...] = fg[...].astype(F32)

    def product_gradient(n):
        columns = pl.ds(n * CC_W, CC_W)
        arrived(gnext.at[:, columns], S_GH + n)
        block = gnext[:, columns] * has_after
        g = ghat[:, columns] + (dot(ef[0, :, TOK:N], block) + dot(ef[1, :, TOK:N], block))
        taps = fhat[:, columns]
        gr, gi, fr, fi = g[:128], g[128:], taps[:128], taps[128:]
        grad_product = inverse(lower, jnp.concatenate([gr * fr + gi * fi, gi * fr - gr * fi], axis=0))
        gk_b[:, columns] = (grad_product * v[:, columns].astype(F32)).astype(BF)
        gv_b[:, columns] = (grad_product * k[:, columns].astype(F32)).astype(BF)

    def share_end():
        for slot, dx in enumerate((0, 3, 1, 2)):
            arrived(share(lax.rem(x + dx, 4) * 2 + (1 - c)), S_X3S + slot)

    def weight_rows(n):
        for t in range(4):
            gather_end(n, t)
        rows = pl.ds(*SPANS[n])
        left = jnp.concatenate([gt[b, rows, :] for b in range(NCTX)], axis=1)
        gw_b[rows, :] = dot(left, cc[...].reshape(NCTX * TOK, COLS)).astype(BF)

    for copy in w_loads:
        copy.wait()
    grad_gated_part(0, 0)
    gated_chunk(0)
    gather_own(0)
    gated_chunk(2)
    gather_own(2)
    gated_chunk(1)
    gather_own(1)
    gated_chunk(3)
    gather_own(3)
    x_near(cot_view, S_COT, S_COTS)
    share_out()
    gather_near(0)
    gather_near(2)
    grad_gated_part(3, 1)
    gather_pass(0, 0)
    gather_pass(2, 0)
    gather_near(1)
    gather_near(3)
    x_far(cot_view, S_COT, S_COTS)
    grad_gated_part(1, 2)
    gather_pass(1, 0)
    gather_pass(3, 0)
    gather_far(0)
    gather_far(2)
    grad_gated_part(2, 3)
    x_near(share, S_X3, S_X3S)
    gather_far(1)
    gather_far(3)
    gradients()
    gather_pass(0, 1)
    gather_pass(2, 1)
    gather_pass(1, 1)
    gather_pass(3, 1)
    filter_terms(0)
    filter_terms(1)
    filter_terms(2)
    filter_terms(3)
    filters_out()
    mixed_part(2)
    gather_pass(0, 2)
    gather_pass(2, 2)
    mixed_far()
    mixed_part(1)
    gather_pass(1, 2)
    gather_pass(3, 2)
    mixed_part(3)
    mixed_near()
    x_far(share, S_X3, S_X3S)
    gather_pass(0, 3)
    gather_pass(2, 3)
    mixed_part(0)
    mixed_last()
    gather_pass(1, 3)
    gather_pass(3, 3)
    filters_sum()
    product_gradient(0)
    product_gradient(1)
    product_gradient(2)
    product_gradient(3)
    share_end()
    weight_rows(0)
    weight_rows(2)
    mixed_end()
    weight_rows(1)
    weight_rows(3)
    filters_end()

    for copy in sends:
        copy.wait_send()

    def sent(d, carry):
        remote(rg.at[0], rg.at[0], S_LG + d, s, sib).wait_send()
        remote(fg.at[rows_of(s), :], fg.at[rows_of(s), :], S_FG + d, s, sib).wait_send()
        return carry

    lax.fori_loop(1, NCTX, sent, 0)
    lax.fori_loop(0, 16, spread_sent, 0)


def write_out(*refs):
    sources, targets, done = refs[:6], refs[6:12], refs[12]
    copies = [pltpu.make_async_copy(a, b, done.at[n]) for n, (a, b) in enumerate(zip(sources, targets))]
    for copy in copies:
        copy.start()
    for copy in copies:
        copy.wait()


def per_device(forward, inverse, query_proj, key_proj, value_proj, filters, out_weight, cotangent):
    sds = jax.ShapeDtypeStruct
    tile = (TOK, CH)
    V = pltpu.VMEM
    anywhere = pl.BlockSpec(memory_space=pltpu.HBM)
    scratch = [
        V(tile, BF), V(tile, BF), V(tile, BF), V((CH, TAPS), BF), V((CH, NCHAN * CH), BF),
        V((NCHAN,) + tile, BF), V((2, N, N), BF), V((2, N, N), BF),
        V((N, CH), BF), V((N, CH), F32), V((N, CH), F32), V((N, CH), F32), V(tile, F32), V(tile, BF),
        V((NCTX, CH, TOK), BF), V((NCTX, TOK, COLS), BF),
        V((4,) + tile, BF), V((4,) + tile, F32), V((4,) + tile, BF), V((6, 64, CH), BF), V((6, 64, CH), BF),
        V(tile, F32), V(tile, BF), V(tile, BF), V((CH, TAPS), BF), V((NCTX, 64, TAPS), BF),
        V((CH, TAPS), BF),
        pltpu.SemaphoreType.DMA((8,)), pltpu.SemaphoreType.DMA((4,)),
        pltpu.SemaphoreType.DMA((N_SEMS,)), pltpu.SemaphoreType.DMA((N_SEMS,)),
    ]
    shapes = [(tile, BF)] * 4 + [((CH, TAPS), F32), ((CH, COLS), BF)]
    inside = pl.BlockSpec(memory_space=pltpu.VMEM)
    results = pl.pallas_call(
        kernel,
        out_shape=tuple(V(shape, dtype) for shape, dtype in shapes),
        in_specs=[anywhere] * 8,
        out_specs=(inside,) * 6,
        scratch_shapes=scratch,
        compiler_params=pltpu.CompilerParams(
            collective_id=0, has_side_effects=True, vmem_limit_bytes=61 * 2**20),
        cost_estimate=pl.CostEstimate(
            flops=7_000_000_000, bytes_accessed=24_000_000, transcendentals=0),
    )(query_proj, key_proj, value_proj, filters, out_weight, cotangent, forward, inverse)
    return pl.pallas_call(
        write_out,
        out_shape=tuple(sds(shape, dtype) for shape, dtype in shapes),
        in_specs=[inside] * 6,
        out_specs=(anywhere,) * 6,
        scratch_shapes=[pltpu.SemaphoreType.DMA((6,))],
        compiler_params=pltpu.CompilerParams(vmem_limit_bytes=4 * 2**20),
    )(*results)


def solution(mesh):
    forward, inverse = transforms()
    placed = (
        P("ctx", "chan"), P("ctx", "chan"), P("ctx", "chan"),
        P("chan", None), P("chan", None), P("ctx", "chan"),
    )

    def body(*args):
        return per_device(jnp.asarray(forward), jnp.asarray(inverse), *args)

    return jax.shard_map(
        body,
        mesh=mesh,
        in_specs=placed,
        out_specs=(
            P("ctx", "chan"), P("ctx", "chan"), P("ctx", "chan"), P("ctx", "chan"),
            P("chan", None), P("chan", "ctx"),
        ),
        check_vma=False,
    )
```
